32 devices in a mesh: tm: 16 (over z, y, core), head: 2 (over x).
Axes of the slice: x: 2, y: 2, z: 4, core: 2. Of those that a mesh axis runs over, the one named last changes fastest.
Arguments:
- frames: bfloat16 [8192, 1024], P('tm'), may hold values from -8 to 8
- norm_gain: float32 [1024], replicated, may hold values from 0.5 to 1.5
- w_qkv: bfloat16 [3, 1024, 1024], P(None, 'tm', 'head'), may hold values from -6 to 6
- slopes: float32 [8], P('head'), may hold values from 3.0517578e-05 to 0.05
- w_out: bfloat16 [1024, 1024], P('head', 'tm'), may hold values from -0.5 to 0.5
Outputs:
- attended: bfloat16 [8192, 1024], P(('tm', 'head'))
The draws below stay inside these ranges and needn't reach their ends.
All inputs are finite; a program needn't handle non-finite values.
Results may differ from the reference program's by a relative error of at most 0.014.
Values may be sent and summed in bfloat16 or wider, within the bound.
A program may use at most 192 MiB of HBM per device.

```python
import math
import jax
import jax.numpy as jnp
from jax import lax

D = 1024
H = 8
HD = 128
FR_DEV = 512
L = 8192


def draw_frames(key, part):
    first = jax.random.fold_in(key, 0)
    values = jax.random.normal(first, (L, D), jnp.float32)
    return jnp.clip(values, -8.0, 8.0).astype(jnp.bfloat16)


def draw_w_qkv(key, part):
    first, second, third = jax.random.split(key, 3)
    inverse = D ** (-0.5)
    w_query = jax.random.normal(first, (D, D), jnp.float32) * inverse
    w_key = jax.random.normal(second, (D, D), jnp.float32) * inverse
    w_value = jax.random.normal(third, (D, D), jnp.float32) * inverse
    stacked = jnp.stack([w_query, w_key, w_value], axis=0)
    return jnp.clip(stacked, -6.0, 6.0).astype(jnp.bfloat16)


def block_scale(rng, extent, pieces, smallest, top_value):
    level, own = 1.0, jax.random.fold_in(rng, 6)
    for dim, parts in pieces:
        heights = jnp.exp(jax.random.uniform(jax.random.fold_in(own, dim), (parts,), jnp.float32, smallest / len(pieces), top_value / len(pieces)))
        level = level * jnp.repeat(heights, extent[dim] // parts).reshape([-1 if axis == dim else 1 for axis in range(len(extent))])
    return level


def normal_values(key, shape, width, reach, cuts=(), kind=jnp.bfloat16):
    entries = width * jax.random.normal(key, shape, jnp.float32)
    if cuts:
        entries = entries * block_scale(key, shape, cuts, -0.22, 0.18)
    return jnp.clip(entries, -reach, reach).astype(kind)


def setup_inputs(seed: int = 0) -> dict:
    key_list = jax.random.split(jax.random.key(seed), 6)
    frames = draw_frames(jax.random.fold_in(key_list[5], 71), 0)
    norm_gain = jnp.clip(1.0 + 0.1 * jax.random.normal(key_list[1], (D,), jnp.float32), 0.5, 1.5)
    w_qkv = draw_w_qkv(jax.random.fold_in(key_list[5], 71), 0)
    slopes = jnp.clip(jnp.exp(math.log(0.05) - 7.4014754 * jax.random.uniform(key_list[3], (H,), jnp.float32) ** block_scale(key_list[3], (H,), ((0, 2),), -0.2, 0.2)), 3.0517578125e-05, 0.05)
    w_out = normal_values(key_list[4], (D, D), HD ** -0.5, 0.5, ((0, 2), (1, 16)))
    return {"frames": frames, "norm_gain": norm_gain, "w_qkv": w_qkv, "slopes": slopes, "w_out": w_out}


def reference(frames, norm_gain, w_qkv, slopes, w_out):
    wide = frames.astype(jnp.float32)
    mean_square = lax.optimization_barrier(jnp.mean(wide * wide, axis=-1, keepdims=True))
    inverse_root = lax.rsqrt(mean_square + 1e-06)
    normed = (wide * inverse_root * norm_gain).astype(jnp.bfloat16)
    query = jnp.dot(normed, w_qkv[0], preferred_element_type=jnp.float32).astype(jnp.bfloat16).reshape(L, H, HD)
    keyed = jnp.dot(normed, w_qkv[1], preferred_element_type=jnp.float32).astype(jnp.bfloat16).reshape(L, H, HD)
    valued = jnp.dot(normed, w_qkv[2], preferred_element_type=jnp.float32).astype(jnp.bfloat16).reshape(L, H, HD)
    key_wide = keyed.astype(jnp.float32)
    value_wide = valued.astype(jnp.float32)
    block = FR_DEV if FR_DEV <= 512 else 512
    count = L // block
    scale = HD ** (-0.5)
    columns = jnp.arange(L, dtype=jnp.int32)

    def one_block(index):
        start = (index * block).astype(jnp.int32)
        query_block = lax.dynamic_slice_in_dim(query, start, block, 0).astype(jnp.float32)
        scores = jnp.einsum('qhd,khd->hqk', query_block, key_wide, precision=lax.Precision.HIGHEST) * scale
        rows_now = start + jnp.arange(block, dtype=jnp.int32)
        differ = (columns[None, :] - rows_now[:, None]) % L
        distance = jnp.minimum(differ, L - differ).astype(jnp.float32)
        scores = scores - slopes[:, None, None] * distance[None, :, :]
        peak = lax.optimization_barrier(jnp.max(scores, axis=-1, keepdims=True))
        expo = jnp.exp(scores - peak)
        totals = lax.optimization_barrier(jnp.sum(expo, axis=-1))
        weights = expo.astype(jnp.bfloat16).astype(jnp.float32)
        numer = jnp.einsum('hqk,khd->qhd', weights, value_wide, precision=lax.Precision.HIGHEST)
        mixed = numer / jnp.transpose(totals)[:, :, None]
        return mixed.astype(jnp.bfloat16).reshape(block, H * HD)
    mixed = lax.map(one_block, jnp.arange(count, dtype=jnp.int32)).reshape(L, H * HD)
    return jnp.dot(mixed, w_out, preferred_element_type=jnp.float32).astype(jnp.bfloat16)
```

```python
import functools
import math
import jax
import jax.numpy as jnp
from jax import lax
from jax.experimental import pallas as pl
from jax.experimental.pallas import tpu as pltpu
from jax.sharding import PartitionSpec as P

MESH = pl.DeviceIdType.MESH
ZS = 4
F32 = jnp.float32
BF16 = jnp.bfloat16


def flip(z, d):
    lo, hi = z % 2, z // 2
    dlo, dhi = d % 2, d // 2
    return (lo + dlo) % 2 + 2 * ((hi + dhi) % 2)


def kernel(
    frames, gain, w, slopes, mixed,
    wbuf, kvbuf, qbuf, kvs, qs, obuf, ost, normed, tiles, acc, peak,
    wz_s, wz_r, wy_s, wy_r, wc_s, wc_r,
    kz_s, kz_r, ky_s, ky_r, kc_s, kc_r,
    qz_s, qz_r, o_s, o_r, l_s,
):
    rows, width = frames.shape
    hd = kvbuf.shape[-1]
    half = rows // 2
    blocks = kvbuf.shape[0]
    tm = lax.axis_index("tm")
    x = lax.axis_index("head")
    z, y, c = tm // 4, (tm // 2) % 2, tm % 2

    def at(zz, yy, cc):
        return zz * 4 + yy * 2 + cc

    def to(index, other=None):
        return (index, x if other is None else other)

    y_peer, c_peer = at(z, 1 - y, c), at(z, y, 1 - c)

    def send(src, dst, ss, rs, dev):
        return pltpu.make_async_remote_copy(
            src_ref=src, dst_ref=dst, send_sem=ss, recv_sem=rs, device_id=dev, device_id_type=MESH
        )

    def w_z(d):
        return send(w, wbuf.at[tm], wz_s.at[d], wz_r.at[d], to(at(flip(z, d), y, c)))

    def w_y(d):
        s = at(flip(z, d), y, c)
        return send(wbuf.at[s], wbuf.at[s], wy_s.at[d], wy_r.at[d], to(y_peer))

    def w_c(d, k):
        s = at(flip(z, d), y if k == 0 else 1 - y, c)
        return send(wbuf.at[s], wbuf.at[s], wc_s.at[d, k], wc_r.at[d, k], to(c_peer))

    def kv_z(d):
        t = flip(z, d)
        return send(kvs.at[t], kvbuf.at[tm], kz_s.at[d], kz_r.at[d], to(at(t, y, c)))

    def kv_y(d):
        s = at(flip(z, d), y, c)
        return send(kvbuf.at[s], kvbuf.at[s], ky_s.at[d], ky_r.at[d], to(y_peer))

    def kv_c(d, k):
        s = at(flip(z, d), y if k == 0 else 1 - y, c)
        return send(kvbuf.at[s], kvbuf.at[s], kc_s.at[d, k], kc_r.at[d, k], to(c_peer))

    def q_z(d):
        t = flip(z, d)
        return send(qs.at[t], qbuf.at[z], qz_s.at[d], qz_r.at[d], to(at(t, y, c)))

    def o_copy(d, k):
        t = flip(z, d)
        xx = x if k == 0 else 1 - x
        return send(
            ost.at[t, xx], obuf.at[x * ZS + z], o_s.at[d, k], o_r.at[d, k], to(at(t, y, c), xx)
        )

    partners = [to(at(flip(z, d), y, c)) for d in (1, 2, 3)] + [to(y_peer), to(c_peer)]
    partners += [to(at(flip(z, d), y, c), 1 - x) for d in range(4)]
    barrier = pltpu.get_barrier_semaphore()
    for dev in partners:
        pl.semaphore_signal(barrier, inc=1, device_id=dev, device_id_type=MESH)
    pl.semaphore_wait(barrier, len(partners))

    for d in (1, 2, 3):
        w_z(d).start()
    wbuf[tm] = w[...]
    w_y(0).start()
    w_c(0, 0).start()

    wide = frames[...].astype(F32)
    inverse_root = lax.rsqrt(jnp.mean(wide * wide, axis=-1, keepdims=True) + 1e-06)
    normed[...] = (wide * inverse_root * gain[...]).astype(BF16)

    log2e = math.log2(math.e)
    slope = slopes[z] * log2e
    ii = lax.broadcasted_iota(jnp.int32, (rows, rows), 0)
    jj = lax.broadcasted_iota(jnp.int32, (rows, rows), 1)
    lin = (ii - jj).astype(F32) * slope
    tiles[0] = -jnp.abs(lin)
    tiles[1] = -lin
    tiles[2] = jnp.abs(lin)
    tiles[3] = lin
    acc[...] = jnp.zeros_like(acc)
    peak[...] = jnp.full_like(peak, -1e30)

    for d in (1, 2, 3):
        w_z(d).wait_recv()
        w_y(d).start()
        w_c(d, 0).start()
    for d in range(4):
        w_y(d).wait_recv()
        w_c(d, 1).start()
    for d in range(4):
        w_c(d, 0).wait_recv()
        w_c(d, 1).wait_recv()

    def project(part):
        weights = wbuf[:, part].reshape(width, ZS * hd)
        return jnp.dot(normed[...], weights, preferred_element_type=F32)

    for part in (1, 2):
        res = project(part).astype(BF16)
        for h in range(ZS):
            kvs[h, part - 1] = res[:, h * hd:(h + 1) * hd]
    for d in (1, 2, 3):
        kv_z(d).start()
    kvbuf[tm] = kvs[z]
    kv_y(0).start()
    kv_c(0, 0).start()
    res = (project(0) * (hd ** -0.5 * log2e)).astype(BF16)
    for h in range(ZS):
        qs[h] = res[:, h * hd:(h + 1) * hd]
    for d in (1, 2, 3):
        q_z(d).start()
    qbuf[z] = qs[z]
    kv_y(0).wait_recv()
    kv_c(0, 1).start()

    ones = jnp.ones((rows, hd), BF16)

    def step(t, carry):
        d, i = t // 4, t % 4
        zk = flip(z, d)
        e = jnp.where(d == 3, 3 - i, i)
        zq = flip(z, e)

        @pl.when(i == 0)
        def _():
            kv_c(d, 0).wait_recv()
            kv_c(d, 1).wait_recv()

        @pl.when(jnp.logical_and(d == 0, i > 0))
        def _():
            q_z(i).wait_recv()

        @pl.when(jnp.logical_and(d < 3, i == 1))
        def _():
            kv_z(d + 1).wait_recv()
            kv_y(d + 1).start()
            kv_c(d + 1, 0).start()

        @pl.when(jnp.logical_and(d < 3, i == 3))
        def _():
            kv_y(d + 1).wait_recv()
            kv_c(d + 1, 1).start()

        me = at(zq, y, c)
        kinds, bases = [], []
        for k in range(4):
            delta = (me - (zk * 4 + k) + blocks) % blocks
            middle = blocks // 2
            kind = jnp.where(
                delta == 0, 0, jnp.where(delta < middle, 1, jnp.where(delta == middle, 2, 3))
            )
            kinds.append(kind)
            far = jnp.where(delta <= middle, delta, blocks - delta) * rows
            bases.append(-slope * far.astype(F32))
        for r in (0, half):
            q = qbuf[zq, r:r + half, :]
            place = pl.ds(pl.multiple_of(zq * rows + r, half), half)
            raw, top = [], None
            for k in range(4):
                s = lax.dot_general(
                    q, kvbuf[zk * 4 + k, 0], (((1,), (1,)), ((), ())), preferred_element_type=F32
                )
                s = s + tiles[kinds[k], r:r + half, :]
                raw.append(s)
                m = s[:, :hd]
                for a in range(hd, rows, hd):
                    m = jnp.maximum(m, s[:, a:a + hd])
                m = m + bases[k]
                top = m if top is None else jnp.maximum(top, m)
            old = peak[place, :]
            new = jnp.maximum(old, jnp.max(top, axis=-1, keepdims=True))
            peak[place, :] = new
            shrink = jnp.exp2(old - new)
            col = new[:, :1]
            total = acc[place, :] * jnp.concatenate([shrink, shrink], axis=1)
            for k in range(4):
                p = jnp.exp2(raw[k] - (col - bases[k])).astype(BF16)
                v = jnp.concatenate([kvbuf[zk * 4 + k, 1], ones], axis=1)
                total = total + jnp.dot(p, v, preferred_element_type=F32)
            acc[place, :] = total

        @pl.when(d == 3)
        def _():
            for s in range(2):
                place = pl.ds(pl.multiple_of(zq * rows + s * half, half), half)
                val = acc[place, :]
                ost[zq, s] = (val[:, :hd] / val[:, hd:]).astype(BF16)
            o_copy(e, 1).start()

        @pl.when(jnp.logical_and(d == 3, e > 0))
        def _():
            o_copy(e, 0).start()

        return carry

    lax.fori_loop(0, 16, step, 0)

    obuf[x * ZS + z] = ost[z, x]
    for d in range(4):
        o_copy(d, 1).wait_recv()
        if d:
            o_copy(d, 0).wait_recv()
    mixed[...] = obuf[...]

    for d in range(4):
        if d:
            w_z(d).wait_send()
            kv_z(d).wait_send()
            q_z(d).wait_send()
            o_copy(d, 0).wait_send()
        w_y(d).wait_send()
        w_c(d, 0).wait_send()
        w_c(d, 1).wait_send()
        kv_y(d).wait_send()
        kv_c(d, 0).wait_send()
        kv_c(d, 1).wait_send()
        o_copy(d, 1).wait_send()


def local_planes(frames, norm_gain, w_qkv, slopes, w_out):
    rows, width = frames.shape
    blocks = lax.axis_size("tm")
    heads = slopes.shape[0]
    hd = w_qkv.shape[2] // heads
    total = heads * lax.axis_size("head")
    half = rows // 2
    w_all = lax.all_gather(w_out, "tm", axis=1, tiled=True)
    w_all = lax.all_gather(w_all, "head", axis=0, tiled=True)
    dma = pltpu.SemaphoreType.DMA
    vmem = pl.BlockSpec(memory_space=pltpu.VMEM)
    mixed = pl.pallas_call(
        kernel,
        out_shape=jax.ShapeDtypeStruct((total, half, hd), BF16),
        in_specs=[vmem, vmem, vmem, pl.BlockSpec(memory_space=pltpu.SMEM)],
        out_specs=vmem,
        scratch_shapes=[
            pltpu.VMEM((blocks,) + w_qkv.shape, BF16),
            pltpu.VMEM((blocks, 2, rows, hd), BF16),
            pltpu.VMEM((ZS, rows, hd), BF16),
            pltpu.VMEM((ZS, 2, rows, hd), BF16),
            pltpu.VMEM((ZS, rows, hd), BF16),
            pltpu.VMEM((total, half, hd), BF16),
            pltpu.VMEM((ZS, 2, half, hd), BF16),
            pltpu.VMEM((rows, width), BF16),
            pltpu.VMEM((4, rows, rows), F32),
            pltpu.VMEM((ZS * rows, 2 * hd), F32),
            pltpu.VMEM((ZS * rows, hd), F32),
        ] + [
            dma((4,)), dma((4,)), dma((4,)), dma((4,)), dma((4, 2)), dma((4, 2)),
            dma((4,)), dma((4,)), dma((4,)), dma((4,)), dma((4, 2)), dma((4, 2)),
            dma((4,)), dma((4,)), dma((4, 2)), dma((4, 2)), dma((1,)),
        ],
        compiler_params=pltpu.CompilerParams(
            collective_id=0, has_side_effects=True, vmem_limit_bytes=56 * 1024 * 1024
        ),
        cost_estimate=pl.CostEstimate(
            flops=11 * 10 ** 9, bytes_accessed=6 * 10 ** 6, transcendentals=17 * 10 ** 6
        ),
    )(frames, norm_gain.reshape(1, -1), w_qkv, slopes)
    flat = jnp.transpose(mixed, (1, 0, 2)).reshape(half, total * hd)
    return jnp.dot(flat, w_all, preferred_element_type=F32).astype(BF16)


def local(frames, norm_gain, w_qkv, slopes, w_out):
    frame_count = frames.shape[0]
    local_heads = slopes.shape[0]
    head_size = w_qkv.shape[2] // local_heads
    tm_count = lax.axis_size("tm")
    clip_len = frame_count * tm_count
    me_tm = lax.axis_index("tm")
    scale = head_size ** (-0.5)
    wide = frames.astype(F32)
    mean_square = jnp.mean(wide * wide, axis=-1, keepdims=True)
    inverse_root = lax.rsqrt(mean_square + 1e-06)
    normed = (wide * inverse_root * norm_gain).astype(BF16)
    projected = jnp.einsum(
        "rd,cde->cre",
        normed,
        lax.all_gather(w_qkv, "tm", axis=1, tiled=True),
        preferred_element_type=F32,
    ).astype(BF16)
    query, keyed, valued = (
        projected[n].reshape(frame_count, local_heads, head_size) for n in range(3)
    )
    row_pos = me_tm * frame_count + jnp.arange(frame_count, dtype=jnp.int32)
    key_piece = lax.all_gather(keyed, "tm", axis=0, tiled=True)
    scores = jnp.einsum("qhd,khd->hqk", query, key_piece, preferred_element_type=F32) * scale
    key_pos = jnp.arange(key_piece.shape[0], dtype=jnp.int32)
    differ = (key_pos[None, :] - row_pos[:, None]) % clip_len
    distance = jnp.minimum(differ, clip_len - differ).astype(F32)
    scores = scores - slopes[:, None, None] * distance[None, :, :]
    expo = jnp.exp(scores - jnp.max(scores, axis=-1, keepdims=True))
    totals = jnp.sum(expo, axis=-1)
    accum = jnp.einsum(
        "hqk,khd->hqd",
        expo.astype(BF16),
        lax.all_gather(valued, "tm", axis=0, tiled=True),
        preferred_element_type=F32,
    )
    mixed = (accum / totals[:, :, None]).astype(BF16)
    mixed = jnp.transpose(mixed, (1, 0, 2)).reshape(frame_count, local_heads * head_size)
    out_local = lax.all_gather(w_out, "tm", axis=1, tiled=True)
    return lax.psum_scatter(
        jnp.dot(mixed, out_local, preferred_element_type=F32).astype(BF16),
        "head",
        scatter_dimension=0,
        tiled=True,
    )


def solution(mesh):
    in_specs = (P("tm", None), P(), P(None, "tm", "head"), P("head"), P("head", "tm"))
    out_specs = P(("tm", "head"), None)
    planes = mesh.shape["tm"] == 4 * ZS and mesh.shape["head"] == 2
    return jax.shard_map(
        local_planes if planes else local,
        mesh=mesh, in_specs=in_specs, out_specs=out_specs, check_vma=False,
    )
```

```python
import math
import jax
import jax.numpy as jnp
from jax import lax
from jax.experimental import pallas as pl
from jax.experimental.pallas import tpu as pltpu
from jax.sharding import PartitionSpec as P

MESH = pl.DeviceIdType.MESH
ZS = 4
F32 = jnp.float32
BF16 = jnp.bfloat16


def flip(z, d):
    lo, hi = z % 2, z // 2
    dlo, dhi = d % 2, d // 2
    return (lo + dlo) % 2 + 2 * ((hi + dhi) % 2)


def kernel(
    frames, gain, w, slopes, w_out, out,
    wbuf, kvbuf, qbuf, kvs, qs, obuf, ost, normed, tiles, acc, peak, wobuf,
    wz_s, wz_r, wy_s, wy_r, wc_s, wc_r,
    kz_s, kz_r, ky_s, ky_r, kc_s, kc_r,
    qz_s, qz_r, o_s, o_r, p_s, p_r,
):
    rows, width = frames.shape
    hd = kvbuf.shape[-1]
    half = rows // 2
    blocks = kvbuf.shape[0]
    tm = lax.axis_index("tm")
    x = lax.axis_index("head")
    z, y, c = tm // 4, (tm // 2) % 2, tm % 2

    def at(zz, yy, cc):
        return zz * 4 + yy * 2 + cc

    def slot(zz, yy, cc):
        return zz * 4 + cc * 2 + yy

    def to(index, other=None):
        return (index, x if other is None else other)

    y_peer, c_peer = at(z, 1 - y, c), at(z, y, 1 - c)

    def send(src, dst, ss, rs, dev):
        return pltpu.make_async_remote_copy(
            src_ref=src, dst_ref=dst, send_sem=ss, recv_sem=rs, device_id=dev, device_id_type=MESH
        )

    def w_z(part, d):
        dev = to(at(flip(z, d), y, c))
        return send(w.at[part], wbuf.at[part, c, y, z], wz_s.at[part, d], wz_r.at[part, d], dev)

    def w_y(part):
        ref = wbuf.at[part, c, y]
        return send(ref, ref, wy_s.at[part], wy_r.at[part], to(y_peer))

    def w_c(part):
        ref = wbuf.at[part, c]
        return send(ref, ref, wc_s.at[part], wc_r.at[part], to(c_peer))

    def kv_z(d, j):
        t = flip(z, d)
        dst = kvbuf.at[slot(z, y, c), j]
        return send(kvs.at[t, j], dst, kz_s.at[d, j], kz_r.at[d, j], to(at(t, y, c)))

    def kv_y(d):
        ref = kvbuf.at[slot(flip(z, d), y, c)]
        return send(ref, ref, ky_s.at[d], ky_r.at[d], to(y_peer))

    def kv_c(d):
        ref = kvbuf.at[pl.ds(slot(flip(z, d), 0, c), 2)]
        return send(ref, ref, kc_s.at[d], kc_r.at[d], to(c_peer))

    def q_z(d):
        t = flip(z, d)
        return send(qs.at[t], qbuf.at[z], qz_s.at[d], qz_r.at[d], to(at(t, y, c)))

    def o_copy(d, k):
        t = flip(z, d)
        xx = x if k == 0 else 1 - x
        return send(
            ost.at[t, xx], obuf.at[x * ZS + z], o_s.at[d, k], o_r.at[d, k], to(at(t, y, c), xx)
        )

    def p_z(d):
        ref = wobuf.at[c, y, x, z]
        return send(ref, ref, p_s.at[d], p_r.at[d], to(at(flip(z, d), y, c)))

    def p_x():
        ref = wobuf.at[c, y, x]
        return send(ref, ref, p_s.at[4], p_r.at[4], to(tm, 1 - x))

    def p_y():
        ref = wobuf.at[c, y]
        return send(ref, ref, p_s.at[5], p_r.at[5], to(y_peer))

    def p_c():
        ref = wobuf.at[c]
        return send(ref, ref, p_s.at[6], p_r.at[6], to(c_peer))

    partners = [to(at(flip(z, d), y, c)) for d in (1, 2, 3)] + [to(y_peer), to(c_peer)]
    partners += [to(at(flip(z, d), y, c), 1 - x) for d in range(4)]
    barrier = pltpu.get_barrier_semaphore()
    for dev in partners:
        pl.semaphore_signal(barrier, inc=1, device_id=dev, device_id_type=MESH)
    pl.semaphore_wait(barrier, len(partners))

    for part in range(3):
        for d in (1, 2, 3):
            w_z(part, d).start()
    for part in range(3):
        wbuf[part, c, y, z] = w[part]
    wobuf[c, y, x, z] = w_out[...]

    wide = frames[...].astype(F32)
    inverse_root = lax.rsqrt(jnp.mean(wide * wide, axis=-1, keepdims=True) + 1e-06)
    normed[...] = (wide * inverse_root * gain[...]).astype(BF16)

    log2e = math.log2(math.e)
    slope = slopes[z] * log2e

    def z_arrived(part):
        for d in (1, 2, 3):
            w_z(part, d).wait_recv()
        w_y(part).start()

    def y_arrived(part):
        w_y(part).wait_recv()
        w_c(part).start()

    def project(part):
        w_c(part).wait_recv()
        weights = jnp.concatenate(
            [wbuf[part, n % 2, (n // 2) % 2, n // 4] for n in range(blocks)], axis=0
        )
        return jnp.dot(normed[...], weights, preferred_element_type=F32)

    z_arrived(0)
    ii = lax.broadcasted_iota(jnp.int32, (rows, rows), 0)
    jj = lax.broadcasted_iota(jnp.int32, (rows, rows), 1)
    lin = (ii - jj).astype(F32) * slope
    tiles[0] = -jnp.abs(lin)
    tiles[1] = -lin
    tiles[2] = jnp.abs(lin)
    tiles[3] = lin
    acc[...] = jnp.zeros_like(acc)
    peak[...] = jnp.full_like(peak, -1e30)
    z_arrived(1)
    y_arrived(0)
    z_arrived(2)
    res = (project(0) * (hd ** -0.5 * log2e)).astype(BF16)
    for h in range(ZS):
        qs[h] = res[:, h * hd:(h + 1) * hd]
    for d in (1, 2, 3):
        q_z(d).start()
    qbuf[z] = qs[z]
    for part in (1, 2):
        y_arrived(part)
        res = project(part).astype(BF16)
        for h in range(ZS):
            kvs[h, part - 1] = res[:, h * hd:(h + 1) * hd]
        for d in (1, 2):
            kv_z(d, part - 1).start()
    kvbuf[slot(z, y, c)] = kvs[z]
    kv_y(0).start()
    for d in (1, 2, 3):
        p_z(d).start()
    kv_y(0).wait_recv()
    kv_c(0).start()

    ones = jnp.ones((rows, hd), BF16)

    def step(t, carry):
        d, i = t // 4, t % 4
        zk = flip(z, d)
        e = jnp.where(d == 3, 3 - i, i)
        zq = flip(z, e)

        @pl.when(i == 0)
        def _():
            kv_c(d).wait_recv()

        @pl.when(jnp.logical_and(d == 0, i > 0))
        def _():
            q_z(i).wait_recv()

        @pl.when(jnp.logical_and(d < 3, i == 1))
        def _():
            kv_z(d + 1, 0).wait_recv()
            kv_z(d + 1, 1).wait_recv()
            kv_y(d + 1).start()

        @pl.when(t == 1)
        def _():
            kv_z(3, 0).start()
            kv_z(3, 1).start()

        @pl.when(jnp.logical_and(d < 3, i == 3))
        def _():
            kv_y(d + 1).wait_recv()
            kv_c(d + 1).start()

        @pl.when(t == 4)
        def _():
            for n in (1, 2, 3):
                p_z(n).wait_recv()
            p_x().start()

        @pl.when(t == 8)
        def _():
            p_x().wait_recv()
            p_y().start()

        @pl.when(t == 12)
        def _():
            p_y().wait_recv()
            p_c().start()

        me = at(zq, y, c)
        kinds, bases = [], []
        for k in range(4):
            delta = (me - at(zk, k % 2, k // 2) + blocks) % blocks
            middle = blocks // 2
            kind = jnp.where(
                delta == 0, 0, jnp.where(delta < middle, 1, jnp.where(delta == middle, 2, 3))
            )
            kinds.append(kind)
            far = jnp.where(delta <= middle, delta, blocks - delta) * rows
            bases.append(-slope * far.astype(F32))
        for r in (0, half):
            q = qbuf[zq, r:r + half, :]
            place = pl.ds(pl.multiple_of(zq * rows + r, half), half)
            raw, top = [], None
            for k in range(4):
                s = lax.dot_general(
                    q, kvbuf[zk * 4 + k, 0], (((1,), (1,)), ((), ())), preferred_element_type=F32
                )
                s = s + tiles[kinds[k], r:r + half, :]
                raw.append(s)
                m = s[:, :hd]
                for a in range(hd, rows, hd):
                    m = jnp.maximum(m, s[:, a:a + hd])
                m = m + bases[k]
                top = m if top is None else jnp.maximum(top, m)
            old = peak[place, :]
            new = jnp.maximum(old, jnp.max(top, axis=-1, keepdims=True))
            peak[place, :] = new
            shrink = jnp.exp2(old - new)
            col = new[:, :1]
            total = acc[place, :] * jnp.concatenate([shrink, shrink], axis=1)
            for k in range(4):
                p = jnp.exp2(raw[k] - (col - bases[k])).astype(BF16)
                v = jnp.concatenate([kvbuf[zk * 4 + k, 1], ones], axis=1)
                total = total + jnp.dot(p, v, preferred_element_type=F32)
            acc[place, :] = total

        @pl.when(d == 3)
        def _():
            for s in range(2):
                place = pl.ds(pl.multiple_of(zq * rows + s * half, half), half)
                val = acc[place, :]
                ost[zq, s] = (val[:, :hd] / val[:, hd:]).astype(BF16)
            o_copy(e, 1).start()

        @pl.when(jnp.logical_and(d == 3, e > 0))
        def _():
            o_copy(e, 0).start()

        return carry

    lax.fori_loop(0, 16, step, 0)

    p_c().wait_recv()
    obuf[x * ZS + z] = ost[z, x]
    for d in (3, 2, 1, 0):
        o_copy(d, 1).wait_recv()
        if d:
            o_copy(d, 0).wait_recv()
    total = None
    for g in range(2):
        mixed = jnp.concatenate([obuf[g * ZS + n] for n in range(ZS)], axis=1)
        weights = jnp.concatenate(
            [wobuf[n % 2, (n // 2) % 2, g, n // 4] for n in range(blocks)], axis=0
        )
        part = lax.dot_general(
            mixed, weights, (((1,), (1,)), ((), ())), preferred_element_type=F32
        )
        total = part if total is None else total + part
    out[...] = total.astype(BF16)

    for part in range(3):
        for d in (1, 2, 3):
            w_z(part, d).wait_send()
        w_y(part).wait_send()
        w_c(part).wait_send()
    for d in range(4):
        if d:
            kv_z(d, 0).wait_send()
            kv_z(d, 1).wait_send()
            q_z(d).wait_send()
            p_z(d).wait_send()
            o_copy(d, 0).wait_send()
        kv_y(d).wait_send()
        kv_c(d).wait_send()
        o_copy(d, 1).wait_send()
    p_x().wait_send()
    p_y().wait_send()
    p_c().wait_send()


def local_planes(frames, norm_gain, w_qkv, slopes, w_out):
    rows, width = frames.shape
    blocks = lax.axis_size("tm")
    heads = slopes.shape[0]
    hd = w_qkv.shape[2] // heads
    total = heads * lax.axis_size("head")
    half = rows // 2
    dma = pltpu.SemaphoreType.DMA
    vmem = pl.BlockSpec(memory_space=pltpu.VMEM)
    return pl.pallas_call(
        kernel,
        out_shape=jax.ShapeDtypeStruct((half, width), BF16),
        in_specs=[vmem, vmem, vmem, pl.BlockSpec(memory_space=pltpu.SMEM), vmem],
        out_specs=vmem,
        scratch_shapes=[
            pltpu.VMEM((3, 2, 2, ZS) + w_qkv.shape[1:], BF16),
            pltpu.VMEM((blocks, 2, rows, hd), BF16),
            pltpu.VMEM((ZS, rows, hd), BF16),
            pltpu.VMEM((ZS, 2, rows, hd), BF16),
            pltpu.VMEM((ZS, rows, hd), BF16),
            pltpu.VMEM((total, half, hd), BF16),
            pltpu.VMEM((ZS, 2, half, hd), BF16),
            pltpu.VMEM((rows, width), BF16),
            pltpu.VMEM((4, rows, rows), F32),
            pltpu.VMEM((ZS * rows, 2 * hd), F32),
            pltpu.VMEM((ZS * rows, hd), F32),
            pltpu.VMEM((2, 2, 2, ZS, w_out.shape[1], w_out.shape[0]), BF16),
        ] + [
            dma((3, 4)), dma((3, 4)), dma((3,)), dma((3,)), dma((3,)), dma((3,)),
            dma((4, 2)), dma((4, 2)), dma((4,)), dma((4,)), dma((4,)), dma((4,)),
            dma((4,)), dma((4,)), dma((4, 2)), dma((4, 2)), dma((7,)), dma((7,)),
        ],
        compiler_params=pltpu.CompilerParams(
            collective_id=0, has_side_effects=True, vmem_limit_bytes=56 * 1024 * 1024
        ),
        cost_estimate=pl.CostEstimate(
            flops=11 * 10 ** 9, bytes_accessed=6 * 10 ** 6, transcendentals=17 * 10 ** 6
        ),
    )(frames, norm_gain.reshape(1, -1), w_qkv, slopes, w_out.T)


def local(frames, norm_gain, w_qkv, slopes, w_out):
    frame_count = frames.shape[0]
    local_heads = slopes.shape[0]
    head_size = w_qkv.shape[2] // local_heads
    tm_count = lax.axis_size("tm")
    clip_len = frame_count * tm_count
    me_tm = lax.axis_index("tm")
    scale = head_size ** (-0.5)
    wide = frames.astype(F32)
    mean_square = jnp.mean(wide * wide, axis=-1, keepdims=True)
    inverse_root = lax.rsqrt(mean_square + 1e-06)
    normed = (wide * inverse_root * norm_gain).astype(BF16)
    projected = jnp.einsum(
        "rd,cde->cre",
        normed,
        lax.all_gather(w_qkv, "tm", axis=1, tiled=True),
        preferred_element_type=F32,
    ).astype(BF16)
    query, keyed, valued = (
        projected[n].reshape(frame_count, local_heads, head_size) for n in range(3)
    )
    row_pos = me_tm * frame_count + jnp.arange(frame_count, dtype=jnp.int32)
    key_piece = lax.all_gather(keyed, "tm", axis=0, tiled=True)
    scores = jnp.einsum("qhd,khd->hqk", query, key_piece, preferred_element_type=F32) * scale
    key_pos = jnp.arange(key_piece.shape[0], dtype=jnp.int32)
    differ = (key_pos[None, :] - row_pos[:, None]) % clip_len
    distance = jnp.minimum(differ, clip_len - differ).astype(F32)
    scores = scores - slopes[:, None, None] * distance[None, :, :]
    expo = jnp.exp(scores - jnp.max(scores, axis=-1, keepdims=True))
    totals = jnp.sum(expo, axis=-1)
    accum = jnp.einsum(
        "hqk,khd->hqd",
        expo.astype(BF16),
        lax.all_gather(valued, "tm", axis=0, tiled=True),
        preferred_element_type=F32,
    )
    mixed = (accum / totals[:, :, None]).astype(BF16)
    mixed = jnp.transpose(mixed, (1, 0, 2)).reshape(frame_count, local_heads * head_size)
    out_local = lax.all_gather(w_out, "tm", axis=1, tiled=True)
    return lax.psum_scatter(
        jnp.dot(mixed, out_local, preferred_element_type=F32).astype(BF16),
        "head",
        scatter_dimension=0,
        tiled=True,
    )


def solution(mesh):
    in_specs = (P("tm", None), P(), P(None, "tm", "head"), P("head"), P("head", "tm"))
    out_specs = P(("tm", "head"), None)
    planes = mesh.shape["tm"] == 4 * ZS and mesh.shape["head"] == 2
    return jax.shard_map(
        local_planes if planes else local,
        mesh=mesh, in_specs=in_specs, out_specs=out_specs, check_vma=False,
    )
```

```python
import math
import jax
import jax.numpy as jnp
from jax import lax
from jax.experimental import pallas as pl
from jax.experimental.pallas import tpu as pltpu
from jax.sharding import PartitionSpec as P

MESH = pl.DeviceIdType.MESH
ZS = 4
F32 = jnp.float32
BF16 = jnp.bfloat16


def flip(z, d):
    lo, hi = z % 2, z // 2
    dlo, dhi = d % 2, d // 2
    return (lo + dlo) % 2 + 2 * ((hi + dhi) % 2)


def kernel(
    frames, gain, w, slopes, w_out, out,
    wbuf, kvbuf, qbuf, kvs, qs, obuf, ost, normed, tiles, acc, peak, wobuf,
    wz_s, wz_r, wy_s, wy_r, wc_s, wc_r,
    kz_s, kz_r, ky_s, ky_r, kc_s, kc_r,
    qz_s, qz_r, o_s, o_r, p_s, p_r,
):
    rows, width = frames.shape
    hd = kvbuf.shape[-1]
    half = rows // 2
    blocks = kvbuf.shape[0]
    tm = lax.axis_index("tm")
    x = lax.axis_index("head")
    z, y, c = tm // 4, (tm // 2) % 2, tm % 2

    def at(zz, yy, cc):
        return zz * 4 + yy * 2 + cc

    def slot(zz, yy, cc):
        return zz * 4 + cc * 2 + yy

    def to(index, other=None):
        return (index, x if other is None else other)

    y_peer, c_peer = at(z, 1 - y, c), at(z, y, 1 - c)

    def send(src, dst, ss, rs, dev):
        return pltpu.make_async_remote_copy(
            src_ref=src, dst_ref=dst, send_sem=ss, recv_sem=rs, device_id=dev, device_id_type=MESH
        )

    def w_z(part, d):
        dev = to(at(flip(z, d), y, c))
        return send(w.at[part], wbuf.at[part, c, y, z], wz_s.at[part, d], wz_r.at[part, d], dev)

    def w_y(part):
        ref = wbuf.at[part, c, y]
        return send(ref, ref, wy_s.at[part], wy_r.at[part], to(y_peer))

    def w_c(part):
        ref = wbuf.at[part, c]
        return send(ref, ref, wc_s.at[part], wc_r.at[part], to(c_peer))

    def kv_z(d, j):
        t = flip(z, d)
        dst = kvbuf.at[slot(z, y, c), j]
        return send(kvs.at[t, j], dst, kz_s.at[d, j], kz_r.at[d, j], to(at(t, y, c)))

    def kv_y(d, j):
        ref = kvbuf.at[slot(flip(z, d), y, c), j]
        return send(ref, ref, ky_s.at[d, j], ky_r.at[d, j], to(y_peer))

    def kv_c(d, j):
        ref = kvbuf.at[pl.ds(slot(flip(z, d), 0, c), 2), j]
        return send(ref, ref, kc_s.at[d, j], kc_r.at[d, j], to(c_peer))

    def q_z(d):
        t = flip(z, d)
        return send(qs.at[t], qbuf.at[z], qz_s.at[d], qz_r.at[d], to(at(t, y, c)))

    def o_copy(d, k):
        t = flip(z, d)
        xx = x if k == 0 else 1 - x
        return send(
            ost.at[t, xx], obuf.at[x * ZS + z], o_s.at[d, k], o_r.at[d, k], to(at(t, y, c), xx)
        )

    def p_z(d):
        ref = wobuf.at[c, y, x, z]
        return send(ref, ref, p_s.at[d], p_r.at[d], to(at(flip(z, d), y, c)))

    def p_x():
        ref = wobuf.at[c, y, x]
        return send(ref, ref, p_s.at[4], p_r.at[4], to(tm, 1 - x))

    def p_y():
        ref = wobuf.at[c, y]
        return send(ref, ref, p_s.at[5], p_r.at[5], to(y_peer))

    def p_c():
        ref = wobuf.at[c]
        return send(ref, ref, p_s.at[6], p_r.at[6], to(c_peer))

    partners = [to(at(flip(z, d), y, c)) for d in (1, 2, 3)] + [to(y_peer), to(c_peer)]
    partners += [to(at(flip(z, d), y, c), 1 - x) for d in range(4)]
    barrier = pltpu.get_barrier_semaphore()
    for dev in partners:
        pl.semaphore_signal(barrier, inc=1, device_id=dev, device_id_type=MESH)
    pl.semaphore_wait(barrier, len(partners))

    for part in (0, 1):
        for d in (1, 2, 3):
            w_z(part, d).start()
    for part in range(3):
        wbuf[part, c, y, z] = w[part]
    wobuf[c, y, x, z] = w_out[...]

    wide = frames[...].astype(F32)
    inverse_root = lax.rsqrt(jnp.mean(wide * wide, axis=-1, keepdims=True) + 1e-06)
    normed[...] = (wide * inverse_root * gain[...]).astype(BF16)

    log2e = math.log2(math.e)
    slope = slopes[z] * log2e

    def z_arrived(part):
        for d in (1, 2, 3):
            w_z(part, d).wait_recv()
        w_y(part).start()

    def y_arrived(part):
        w_y(part).wait_recv()
        w_c(part).start()

    def project(part):
        w_c(part).wait_recv()
        weights = jnp.concatenate(
            [wbuf[part, n % 2, (n // 2) % 2, n // 4] for n in range(blocks)], axis=0
        )
        return jnp.dot(normed[...], weights, preferred_element_type=F32)

    z_arrived(0)
    for d in (1, 2, 3):
        w_z(2, d).start()
    ii = lax.broadcasted_iota(jnp.int32, (rows, rows), 0)
    jj = lax.broadcasted_iota(jnp.int32, (rows, rows), 1)
    lin = (ii - jj).astype(F32) * slope
    tiles[0] = -jnp.abs(lin)
    tiles[1] = -lin
    tiles[2] = jnp.abs(lin)
    tiles[3] = lin
    acc[...] = jnp.zeros_like(acc)
    peak[...] = jnp.full_like(peak, -1e30)
    z_arrived(1)
    y_arrived(0)
    z_arrived(2)
    res = (project(0) * (hd ** -0.5 * log2e)).astype(BF16)
    for h in range(ZS):
        qs[h] = res[:, h * hd:(h + 1) * hd]
    for d in (1, 2, 3):
        q_z(d).start()
    qbuf[z] = qs[z]
    mine = slot(z, y, c)
    for part in (1, 2):
        y_arrived(part)
        res = project(part)
        for h in range(ZS):
            piece = res[:, h * hd:(h + 1) * hd]
            if part == 1:
                for a in range(0, rows, hd):
                    kvs[h, 0, a:a + hd, :] = piece[a:a + hd, :].T.astype(BF16)
            else:
                kvs[h, 1] = piece.astype(BF16)
        for d in (1, 2):
            kv_z(d, part - 1).start()
        kvbuf[mine, part - 1] = kvs[z, part - 1]
        kv_y(0, part - 1).start()
    for d in (1, 2, 3):
        p_z(d).start()
    for j in range(2):
        kv_y(0, j).wait_recv()
        kv_c(0, j).start()

    ones = jnp.ones((rows, hd), BF16)

    def step(t, carry):
        d, i = t // 4, t % 4
        zk = flip(z, d)
        e = jnp.where(d == 3, 3 - i, i)
        zq = flip(z, e)

        @pl.when(i == 0)
        def _():
            kv_c(d, 0).wait_recv()
            kv_c(d, 1).wait_recv()

        @pl.when(jnp.logical_and(d == 0, i > 0))
        def _():
            q_z(i).wait_recv()

        @pl.when(jnp.logical_and(d < 3, i == 1))
        def _():
            for j in range(2):
                kv_z(d + 1, j).wait_recv()
                kv_y(d + 1, j).start()

        @pl.when(t == 1)
        def _():
            kv_z(3, 0).start()
            kv_z(3, 1).start()

        @pl.when(jnp.logical_and(d < 3, i == 3))
        def _():
            for j in range(2):
                kv_y(d + 1, j).wait_recv()
                kv_c(d + 1, j).start()

        @pl.when(t == 4)
        def _():
            for n in (1, 2, 3):
                p_z(n).wait_recv()
            p_x().start()

        @pl.when(t == 8)
        def _():
            p_x().wait_recv()
            p_y().start()

        @pl.when(t == 12)
        def _():
            p_y().wait_recv()
            p_c().start()

        me = at(zq, y, c)
        kinds, bases = [], []
        for k in range(4):
            delta = (me - at(zk, k % 2, k // 2) + blocks) % blocks
            middle = blocks // 2
            kind = jnp.where(
                delta == 0, 0, jnp.where(delta < middle, 1, jnp.where(delta == middle, 2, 3))
            )
            kinds.append(kind)
            far = jnp.where(delta <= middle, delta, blocks - delta) * rows
            bases.append(-slope * far.astype(F32))
        def score(r, k):
            keys = kvbuf[zk * 4 + k, 0]
            keys = jnp.concatenate([keys[a:a + hd] for a in range(0, rows, hd)], axis=1)
            s = jnp.dot(qbuf[zq, r:r + half, :], keys, preferred_element_type=F32)
            s = s + tiles[kinds[k], r:r + half, :]
            m = s[:, :hd]
            for a in range(hd, rows, hd):
                m = jnp.maximum(m, s[:, a:a + hd])
            return s, m + bases[k]

        def begin(r, tops):
            place = pl.ds(pl.multiple_of(zq * rows + r, half), half)
            top = jnp.maximum(jnp.maximum(tops[0], tops[1]), jnp.maximum(tops[2], tops[3]))
            old = peak[place, :]
            new = jnp.maximum(old, jnp.max(top, axis=-1, keepdims=True))
            peak[place, :] = new
            shrink = jnp.exp2(old - new)
            return new[:, :1], acc[place, :] * jnp.concatenate([shrink, shrink], axis=1)

        def add(total, s, col, k):
            p = jnp.exp2(s - (col - bases[k])).astype(BF16)
            v = jnp.concatenate([kvbuf[zk * 4 + k, 1], ones], axis=1)
            return total + jnp.dot(p, v, preferred_element_type=F32)

        def finish(r, total):
            acc[pl.ds(pl.multiple_of(zq * rows + r, half), half), :] = total

        first = [score(0, k) for k in range(4)]
        col, total = begin(0, [m for _, m in first])
        second = []
        for k in range(4):
            second.append(score(half, k))
            total = add(total, first[k][0], col, k)
        finish(0, total)
        col, total = begin(half, [m for _, m in second])
        for k in range(4):
            total = add(total, second[k][0], col, k)
        finish(half, total)

        @pl.when(d == 3)
        def _():
            for s in range(2):
                place = pl.ds(pl.multiple_of(zq * rows + s * half, half), half)
                val = acc[place, :]
                ost[zq, s] = (val[:, :hd] / val[:, hd:]).astype(BF16)
            o_copy(e, 1).start()

        @pl.when(jnp.logical_and(d == 3, e > 0))
        def _():
            o_copy(e, 0).start()

        return carry

    lax.fori_loop(0, 16, step, 0)

    p_c().wait_recv()
    obuf[x * ZS + z] = ost[z, x]
    for d in (3, 2, 1, 0):
        o_copy(d, 1).wait_recv()
        if d:
            o_copy(d, 0).wait_recv()
    total = None
    for g in range(2):
        mixed = jnp.concatenate([obuf[g * ZS + n] for n in range(ZS)], axis=1)
        weights = jnp.concatenate(
            [wobuf[n % 2, (n // 2) % 2, g, n // 4] for n in range(blocks)], axis=0
        )
        part = lax.dot_general(
            mixed, weights, (((1,), (1,)), ((), ())), preferred_element_type=F32
        )
        total = part if total is None else total + part
    out[...] = total.astype(BF16)

    for part in range(3):
        for d in (1, 2, 3):
            w_z(part, d).wait_send()
        w_y(part).wait_send()
        w_c(part).wait_send()
    for d in range(4):
        if d:
            kv_z(d, 0).wait_send()
            kv_z(d, 1).wait_send()
            q_z(d).wait_send()
            p_z(d).wait_send()
            o_copy(d, 0).wait_send()
        for j in range(2):
            kv_y(d, j).wait_send()
            kv_c(d, j).wait_send()
        o_copy(d, 1).wait_send()
    p_x().wait_send()
    p_y().wait_send()
    p_c().wait_send()


def local_planes(frames, norm_gain, w_qkv, slopes, w_out):
    rows, width = frames.shape
    blocks = lax.axis_size("tm")
    heads = slopes.shape[0]
    hd = w_qkv.shape[2] // heads
    total = heads * lax.axis_size("head")
    half = rows // 2
    dma = pltpu.SemaphoreType.DMA
    vmem = pl.BlockSpec(memory_space=pltpu.VMEM)
    return pl.pallas_call(
        kernel,
        out_shape=jax.ShapeDtypeStruct((half, width), BF16),
        in_specs=[vmem, vmem, vmem, pl.BlockSpec(memory_space=pltpu.SMEM), vmem],
        out_specs=vmem,
        scratch_shapes=[
            pltpu.VMEM((3, 2, 2, ZS) + w_qkv.shape[1:], BF16),
            pltpu.VMEM((blocks, 2, rows, hd), BF16),
            pltpu.VMEM((ZS, rows, hd), BF16),
            pltpu.VMEM((ZS, 2, rows, hd), BF16),
            pltpu.VMEM((ZS, rows, hd), BF16),
            pltpu.VMEM((total, half, hd), BF16),
            pltpu.VMEM((ZS, 2, half, hd), BF16),
            pltpu.VMEM((rows, width), BF16),
            pltpu.VMEM((4, rows, rows), F32),
            pltpu.VMEM((ZS * rows, 2 * hd), F32),
            pltpu.VMEM((ZS * rows, hd), F32),
            pltpu.VMEM((2, 2, 2, ZS, w_out.shape[1], w_out.shape[0]), BF16),
        ] + [
            dma((3, 4)), dma((3, 4)), dma((3,)), dma((3,)), dma((3,)), dma((3,)),
            dma((4, 2)), dma((4, 2)), dma((4, 2)), dma((4, 2)), dma((4, 2)), dma((4, 2)),
            dma((4,)), dma((4,)), dma((4, 2)), dma((4, 2)), dma((7,)), dma((7,)),
        ],
        compiler_params=pltpu.CompilerParams(
            collective_id=0, has_side_effects=True, vmem_limit_bytes=56 * 1024 * 1024
        ),
        cost_estimate=pl.CostEstimate(
            flops=11 * 10 ** 9, bytes_accessed=6 * 10 ** 6, transcendentals=17 * 10 ** 6
        ),
    )(frames, norm_gain.reshape(1, -1), w_qkv, slopes, w_out.T)


def local(frames, norm_gain, w_qkv, slopes, w_out):
    frame_count = frames.shape[0]
    local_heads = slopes.shape[0]
    head_size = w_qkv.shape[2] // local_heads
    tm_count = lax.axis_size("tm")
    clip_len = frame_count * tm_count
    me_tm = lax.axis_index("tm")
    scale = head_size ** (-0.5)
    wide = frames.astype(F32)
    mean_square = jnp.mean(wide * wide, axis=-1, keepdims=True)
    inverse_root = lax.rsqrt(mean_square + 1e-06)
    normed = (wide * inverse_root * norm_gain).astype(BF16)
    projected = jnp.einsum(
        "rd,cde->cre",
        normed,
        lax.all_gather(w_qkv, "tm", axis=1, tiled=True),
        preferred_element_type=F32,
    ).astype(BF16)
    query, keyed, valued = (
        projected[n].reshape(frame_count, local_heads, head_size) for n in range(3)
    )
    row_pos = me_tm * frame_count + jnp.arange(frame_count, dtype=jnp.int32)
    key_piece = lax.all_gather(keyed, "tm", axis=0, tiled=True)
    scores = jnp.einsum("qhd,khd->hqk", query, key_piece, preferred_element_type=F32) * scale
    key_pos = jnp.arange(key_piece.shape[0], dtype=jnp.int32)
    differ = (key_pos[None, :] - row_pos[:, None]) % clip_len
    distance = jnp.minimum(differ, clip_len - differ).astype(F32)
    scores = scores - slopes[:, None, None] * distance[None, :, :]
    expo = jnp.exp(scores - jnp.max(scores, axis=-1, keepdims=True))
    totals = jnp.sum(expo, axis=-1)
    accum = jnp.einsum(
        "hqk,khd->hqd",
        expo.astype(BF16),
        lax.all_gather(valued, "tm", axis=0, tiled=True),
        preferred_element_type=F32,
    )
    mixed = (accum / totals[:, :, None]).astype(BF16)
    mixed = jnp.transpose(mixed, (1, 0, 2)).reshape(frame_count, local_heads * head_size)
    out_local = lax.all_gather(w_out, "tm", axis=1, tiled=True)
    return lax.psum_scatter(
        jnp.dot(mixed, out_local, preferred_element_type=F32).astype(BF16),
        "head",
        scatter_dimension=0,
        tiled=True,
    )


def solution(mesh):
    in_specs = (P("tm", None), P(), P(None, "tm", "head"), P("head"), P("head", "tm"))
    out_specs = P(("tm", "head"), None)
    planes = mesh.shape["tm"] == 4 * ZS and mesh.shape["head"] == 2
    return jax.shard_map(
        local_planes if planes else local,
        mesh=mesh, in_specs=in_specs, out_specs=out_specs, check_vma=False,
    )
```

```python
import math
import jax
import jax.numpy as jnp
from jax import lax
from jax.experimental import pallas as pl
from jax.experimental.pallas import tpu as pltpu
from jax.sharding import PartitionSpec as P

MESH = pl.DeviceIdType.MESH
ZS = 4
F32 = jnp.float32
BF16 = jnp.bfloat16


def flip(z, d):
    lo, hi = z % 2, z // 2
    dlo, dhi = d % 2, d // 2
    return (lo + dlo) % 2 + 2 * ((hi + dhi) % 2)


def kernel(
    frames, gain, w, slopes, w_out, out,
    wbuf, kvbuf, qbuf, kvs, qs, obuf, ost, normed, tiles, acc, peak, wobuf,
    wz_s, wz_r, wy_s, wy_r, wc_s, wc_r,
    kz_s, kz_r, ky_s, ky_r, kc_s, kc_r,
    qz_s, qz_r, o_s, o_r, p_s, p_r,
):
    rows, width = frames.shape
    hd = kvbuf.shape[-1]
    half = rows // 2
    blocks = kvbuf.shape[0]
    tm = lax.axis_index("tm")
    x = lax.axis_index("head")
    z, y, c = tm // 4, (tm // 2) % 2, tm % 2

    def at(zz, yy, cc):
        return zz * 4 + yy * 2 + cc

    def slot(zz, yy, cc):
        return zz * 4 + cc * 2 + yy

    def to(index, other=None):
        return (index, x if other is None else other)

    y_peer, c_peer = at(z, 1 - y, c), at(z, y, 1 - c)

    def send(src, dst, ss, rs, dev):
        return pltpu.make_async_remote_copy(
            src_ref=src, dst_ref=dst, send_sem=ss, recv_sem=rs, device_id=dev, device_id_type=MESH
        )

    inner = jnp.logical_or(z == 1, z == 2)
    outer = jnp.logical_or(z == 0, z == 3)

    def w_z(part, d):
        if d == 0:
            src, dst, t = w.at[part], wbuf.at[part, c, y, z], flip(z, 1)
        else:
            near = z // 2
            src = wbuf.at[part, c, y, pl.ds(2 * (near if d == 1 else 1 - near), 2)]
            dst, t = src, (3 - z if d == 1 else flip(z, 1))
        dev = to(at(t, y, c))
        return send(src, dst, wz_s.at[part, d], wz_r.at[part, d], dev)

    def w_y(part):
        ref = wbuf.at[part, c, y]
        return send(ref, ref, wy_s.at[part], wy_r.at[part], to(y_peer))

    def w_c(part):
        ref = wbuf.at[part, c]
        return send(ref, ref, wc_s.at[part], wc_r.at[part], to(c_peer))

    def kv_z(d, j):
        t = flip(z, d)
        dst = kvbuf.at[slot(z, y, c), j]
        return send(kvs.at[t, j], dst, kz_s.at[d, j], kz_r.at[d, j], to(at(t, y, c)))

    def kv_y(d, j):
        ref = kvbuf.at[slot(flip(z, d), y, c), j]
        return send(ref, ref, ky_s.at[d, j], ky_r.at[d, j], to(y_peer))

    def kv_c(d, j):
        ref = kvbuf.at[pl.ds(slot(flip(z, d), 0, c), 2), j]
        return send(ref, ref, kc_s.at[d, j], kc_r.at[d, j], to(c_peer))

    def q_z(d):
        t = flip(z, d)
        return send(qs.at[t], qbuf.at[z], qz_s.at[d], qz_r.at[d], to(at(t, y, c)))

    def o_copy(d, k):
        t = flip(z, d)
        xx = x if k == 0 else 1 - x
        return send(
            ost.at[t, xx], obuf.at[x * ZS + z], o_s.at[d, k], o_r.at[d, k], to(at(t, y, c), xx)
        )

    def p_z(d):
        ref = wobuf.at[c, y, x, z]
        return send(ref, ref, p_s.at[d], p_r.at[d], to(at(flip(z, d), y, c)))

    def p_x():
        ref = wobuf.at[c, y, x]
        return send(ref, ref, p_s.at[4], p_r.at[4], to(tm, 1 - x))

    def p_y():
        ref = wobuf.at[c, y]
        return send(ref, ref, p_s.at[5], p_r.at[5], to(y_peer))

    def p_c():
        ref = wobuf.at[c]
        return send(ref, ref, p_s.at[6], p_r.at[6], to(c_peer))

    partners = [to(at(flip(z, d), y, c)) for d in (1, 2, 3)] + [to(y_peer), to(c_peer)]
    partners += [to(at(flip(z, d), y, c), 1 - x) for d in range(4)]
    barrier = pltpu.get_barrier_semaphore()
    for dev in partners:
        pl.semaphore_signal(barrier, inc=1, device_id=dev, device_id_type=MESH)
    pl.semaphore_wait(barrier, len(partners))

    for part in range(3):
        w_z(part, 0).start()
    for part in range(3):
        wbuf[part, c, y, z] = w[part]
    wobuf[c, y, x, z] = w_out[...]

    log2e = math.log2(math.e)
    slope = slopes[z] * log2e

    def z_near(part):
        w_z(part, 0).wait_recv()

        @pl.when(inner)
        def _():
            w_z(part, 1).start()

    def z_arrived(part):
        @pl.when(inner)
        def _():
            w_z(part, 1).wait_recv()
            w_z(part, 2).start()

        @pl.when(outer)
        def _():
            w_z(part, 2).wait_recv()

        w_y(part).start()

    def y_arrived(part):
        w_y(part).wait_recv()
        w_c(part).start()

    def project(part):
        w_c(part).wait_recv()
        weights = jnp.concatenate(
            [wbuf[part, n % 2, (n // 2) % 2, n // 4] for n in range(blocks)], axis=0
        )
        return jnp.dot(normed[...], weights, preferred_element_type=F32)

    z_near(0)
    z_near(1)
    z_near(2)
    wide = frames[...].astype(F32)
    inverse_root = lax.rsqrt(jnp.mean(wide * wide, axis=-1, keepdims=True) + 1e-06)
    normed[...] = (wide * inverse_root * gain[...]).astype(BF16)

    z_arrived(0)
    ii = lax.broadcasted_iota(jnp.int32, (rows, rows), 0)
    jj = lax.broadcasted_iota(jnp.int32, (rows, rows), 1)
    lin = (ii - jj).astype(F32) * slope
    tiles[0] = -jnp.abs(lin)
    tiles[1] = -lin
    tiles[2] = jnp.abs(lin)
    tiles[3] = lin
    acc[...] = jnp.zeros_like(acc)
    peak[...] = jnp.full_like(peak, -1e30)
    z_arrived(1)
    y_arrived(0)
    z_arrived(2)
    for d in (2, 3, 1):
        p_z(d).start()
    res = (project(0) * (hd ** -0.5 * log2e)).astype(BF16)
    for h in range(ZS):
        qs[h] = res[:, h * hd:(h + 1) * hd]
    for d in (2, 3, 1):
        q_z(d).start()
    qbuf[z] = qs[z]
    mine = slot(z, y, c)
    for part in (1, 2):
        y_arrived(part)
        res = project(part)
        for h in range(ZS):
            piece = res[:, h * hd:(h + 1) * hd]
            if part == 1:
                for a in range(0, rows, hd):
                    kvs[h, 0, a:a + hd, :] = piece[a:a + hd, :].T.astype(BF16)
            else:
                kvs[h, 1] = piece.astype(BF16)
        for d in (2, 1):
            kv_z(d, part - 1).start()
        kvbuf[mine, part - 1] = kvs[z, part - 1]
        kv_y(0, part - 1).start()
    for j in range(2):
        kv_y(0, j).wait_recv()
        kv_c(0, j).start()
    kv_z(2, 0).wait_send()
    kv_z(3, 0).start()

    ones = jnp.ones((rows, hd), BF16)

    def step(t, carry):
        d, i = t // 4, t % 4
        zk = flip(z, d)
        e = jnp.where(d == 3, 3 - i, i)
        zq = flip(z, e)

        @pl.when(i == 0)
        def _():
            kv_c(d, 0).wait_recv()
            kv_c(d, 1).wait_recv()

        @pl.when(jnp.logical_and(d == 0, i > 0))
        def _():
            q_z(i).wait_recv()

        @pl.when(jnp.logical_and(d < 3, i == 1))
        def _():
            for j in range(2):
                kv_z(d + 1, j).wait_recv()
                kv_y(d + 1, j).start()

        @pl.when(t == 1)
        def _():
            kv_z(2, 1).wait_send()
            kv_z(3, 1).start()

        @pl.when(jnp.logical_and(d < 3, i == 3))
        def _():
            for j in range(2):
                kv_y(d + 1, j).wait_recv()
                kv_c(d + 1, j).start()

        @pl.when(t == 4)
        def _():
            for n in (1, 2, 3):
                p_z(n).wait_recv()
            p_x().start()

        @pl.when(t == 8)
        def _():
            p_x().wait_recv()
            p_y().start()

        @pl.when(t == 12)
        def _():
            p_y().wait_recv()
            p_c().start()

        me = at(zq, y, c)
        kinds, bases = [], []
        for k in range(4):
            delta = (me - at(zk, k % 2, k // 2) + blocks) % blocks
            middle = blocks // 2
            kind = jnp.where(
                delta == 0, 0, jnp.where(delta < middle, 1, jnp.where(delta == middle, 2, 3))
            )
            kinds.append(kind)
            far = jnp.where(delta <= middle, delta, blocks - delta) * rows
            bases.append(-slope * far.astype(F32))
        def score(r, k):
            keys = kvbuf[zk * 4 + k, 0]
            keys = jnp.concatenate([keys[a:a + hd] for a in range(0, rows, hd)], axis=1)
            s = jnp.dot(qbuf[zq, r:r + half, :], keys, preferred_element_type=F32)
            s = s + tiles[kinds[k], r:r + half, :]
            m = s[:, :hd]
            for a in range(hd, rows, hd):
                m = jnp.maximum(m, s[:, a:a + hd])
            return s, m + bases[k]

        def begin(r, tops):
            place = pl.ds(pl.multiple_of(zq * rows + r, half), half)
            top = jnp.maximum(jnp.maximum(tops[0], tops[1]), jnp.maximum(tops[2], tops[3]))
            old = peak[place, :]
            new = jnp.maximum(old, jnp.max(top, axis=-1, keepdims=True))
            peak[place, :] = new
            shrink = jnp.exp2(old - new)
            return new[:, :1], acc[place, :] * jnp.concatenate([shrink, shrink], axis=1)

        def add(total, s, col, k):
            p = jnp.exp2(s - (col - bases[k])).astype(BF16)
            v = jnp.concatenate([kvbuf[zk * 4 + k, 1], ones], axis=1)
            return total + jnp.dot(p, v, preferred_element_type=F32)

        def finish(r, total):
            acc[pl.ds(pl.multiple_of(zq * rows + r, half), half), :] = total

        first = [score(0, k) for k in range(4)]
        col, total = begin(0, [m for _, m in first])
        second = []
        for k in range(4):
            second.append(score(half, k))
            total = add(total, first[k][0], col, k)
        finish(0, total)
        col, total = begin(half, [m for _, m in second])
        for k in range(4):
            total = add(total, second[k][0], col, k)
        finish(half, total)

        @pl.when(d == 3)
        def _():
            for s in range(2):
                place = pl.ds(pl.multiple_of(zq * rows + s * half, half), half)
                val = acc[place, :]
                ost[zq, s] = (val[:, :hd] / val[:, hd:]).astype(BF16)
            o_copy(e, 1).start()

        @pl.when(jnp.logical_and(d == 3, e > 0))
        def _():
            o_copy(e, 0).start()

        return carry

    lax.fori_loop(0, 16, step, 0)

    p_c().wait_recv()
    obuf[x * ZS + z] = ost[z, x]
    for d in (3, 2, 1, 0):
        o_copy(d, 1).wait_recv()
        if d:
            o_copy(d, 0).wait_recv()
    total = None
    for g in range(2):
        mixed = jnp.concatenate([obuf[g * ZS + n] for n in range(ZS)], axis=1)
        weights = jnp.concatenate(
            [wobuf[n % 2, (n // 2) % 2, g, n // 4] for n in range(blocks)], axis=0
        )
        part = lax.dot_general(
            mixed, weights, (((1,), (1,)), ((), ())), preferred_element_type=F32
        )
        total = part if total is None else total + part
    out[...] = total.astype(BF16)

    for part in range(3):
        w_z(part, 0).wait_send()

        @pl.when(inner)
        def _():
            w_z(part, 1).wait_send()
            w_z(part, 2).wait_send()

        w_y(part).wait_send()
        w_c(part).wait_send()
    for d in range(4):
        if d:
            if d != 2:
                kv_z(d, 0).wait_send()
                kv_z(d, 1).wait_send()
            q_z(d).wait_send()
            p_z(d).wait_send()
            o_copy(d, 0).wait_send()
        for j in range(2):
            kv_y(d, j).wait_send()
            kv_c(d, j).wait_send()
        o_copy(d, 1).wait_send()
    p_x().wait_send()
    p_y().wait_send()
    p_c().wait_send()


def local_planes(frames, norm_gain, w_qkv, slopes, w_out):
    rows, width = frames.shape
    blocks = lax.axis_size("tm")
    heads = slopes.shape[0]
    hd = w_qkv.shape[2] // heads
    total = heads * lax.axis_size("head")
    half = rows // 2
    dma = pltpu.SemaphoreType.DMA
    vmem = pl.BlockSpec(memory_space=pltpu.VMEM)
    return pl.pallas_call(
        kernel,
        out_shape=jax.ShapeDtypeStruct((half, width), BF16),
        in_specs=[vmem, vmem, vmem, pl.BlockSpec(memory_space=pltpu.SMEM), vmem],
        out_specs=vmem,
        scratch_shapes=[
            pltpu.VMEM((3, 2, 2, ZS) + w_qkv.shape[1:], BF16),
            pltpu.VMEM((blocks, 2, rows, hd), BF16),
            pltpu.VMEM((ZS, rows, hd), BF16),
            pltpu.VMEM((ZS, 2, rows, hd), BF16),
            pltpu.VMEM((ZS, rows, hd), BF16),
            pltpu.VMEM((total, half, hd), BF16),
            pltpu.VMEM((ZS, 2, half, hd), BF16),
            pltpu.VMEM((rows, width), BF16),
            pltpu.VMEM((4, rows, rows), F32),
            pltpu.VMEM((ZS * rows, 2 * hd), F32),
            pltpu.VMEM((ZS * rows, hd), F32),
            pltpu.VMEM((2, 2, 2, ZS, w_out.shape[1], w_out.shape[0]), BF16),
        ] + [
            dma((3, 4)), dma((3, 4)), dma((3,)), dma((3,)), dma((3,)), dma((3,)),
            dma((4, 2)), dma((4, 2)), dma((4, 2)), dma((4, 2)), dma((4, 2)), dma((4, 2)),
            dma((4,)), dma((4,)), dma((4, 2)), dma((4, 2)), dma((7,)), dma((7,)),
        ],
        compiler_params=pltpu.CompilerParams(
            collective_id=0, has_side_effects=True, vmem_limit_bytes=56 * 1024 * 1024
        ),
        cost_estimate=pl.CostEstimate(
            flops=11 * 10 ** 9, bytes_accessed=6 * 10 ** 6, transcendentals=17 * 10 ** 6
        ),
    )(frames, norm_gain.reshape(1, -1), w_qkv, slopes, w_out.T)


def local(frames, norm_gain, w_qkv, slopes, w_out):
    frame_count = frames.shape[0]
    local_heads = slopes.shape[0]
    head_size = w_qkv.shape[2] // local_heads
    tm_count = lax.axis_size("tm")
    clip_len = frame_count * tm_count
    me_tm = lax.axis_index("tm")
    scale = head_size ** (-0.5)
    wide = frames.astype(F32)
    mean_square = jnp.mean(wide * wide, axis=-1, keepdims=True)
    inverse_root = lax.rsqrt(mean_square + 1e-06)
    normed = (wide * inverse_root * norm_gain).astype(BF16)
    projected = jnp.einsum(
        "rd,cde->cre",
        normed,
        lax.all_gather(w_qkv, "tm", axis=1, tiled=True),
        preferred_element_type=F32,
    ).astype(BF16)
    query, keyed, valued = (
        projected[n].reshape(frame_count, local_heads, head_size) for n in range(3)
    )
    row_pos = me_tm * frame_count + jnp.arange(frame_count, dtype=jnp.int32)
    key_piece = lax.all_gather(keyed, "tm", axis=0, tiled=True)
    scores = jnp.einsum("qhd,khd->hqk", query, key_piece, preferred_element_type=F32) * scale
    key_pos = jnp.arange(key_piece.shape[0], dtype=jnp.int32)
    differ = (key_pos[None, :] - row_pos[:, None]) % clip_len
    distance = jnp.minimum(differ, clip_len - differ).astype(F32)
    scores = scores - slopes[:, None, None] * distance[None, :, :]
    expo = jnp.exp(scores - jnp.max(scores, axis=-1, keepdims=True))
    totals = jnp.sum(expo, axis=-1)
    accum = jnp.einsum(
        "hqk,khd->hqd",
        expo.astype(BF16),
        lax.all_gather(valued, "tm", axis=0, tiled=True),
        preferred_element_type=F32,
    )
    mixed = (accum / totals[:, :, None]).astype(BF16)
    mixed = jnp.transpose(mixed, (1, 0, 2)).reshape(frame_count, local_heads * head_size)
    out_local = lax.all_gather(w_out, "tm", axis=1, tiled=True)
    return lax.psum_scatter(
        jnp.dot(mixed, out_local, preferred_element_type=F32).astype(BF16),
        "head",
        scatter_dimension=0,
        tiled=True,
    )


def solution(mesh):
    in_specs = (P("tm", None), P(), P(None, "tm", "head"), P("head"), P("head", "tm"))
    out_specs = P(("tm", "head"), None)
    planes = mesh.shape["tm"] == 4 * ZS and mesh.shape["head"] == 2
    return jax.shard_map(
        local_planes if planes else local,
        mesh=mesh, in_specs=in_specs, out_specs=out_specs, check_vma=False,
    )
```

```python
import math
import jax
import jax.numpy as jnp
from jax import lax
from jax.experimental import pallas as pl
from jax.experimental.pallas import tpu as pltpu
from jax.sharding import PartitionSpec as P

MESH = pl.DeviceIdType.MESH
ZS = 4
F32 = jnp.float32
BF16 = jnp.bfloat16


def flip(z, d):
    lo, hi = z % 2, z // 2
    dlo, dhi = d % 2, d // 2
    return (lo + dlo) % 2 + 2 * ((hi + dhi) % 2)


def kernel(
    frames, gain, w, slopes, w_out, out,
    wbuf, kvbuf, qbuf, kvs, qs, obuf, ost, normed, tiles, acc, peak, wobuf,
    wz_s, wz_r, wy_s, wy_r, wc_s, wc_r,
    kz_s, kz_r, ky_s, ky_r, kc_s, kc_r,
    qz_s, qz_r, o_s, o_r, p_s, p_r,
):
    rows, width = frames.shape
    hd = kvbuf.shape[-1]
    half = rows // 2
    blocks = kvbuf.shape[0]
    tm = lax.axis_index("tm")
    x = lax.axis_index("head")
    z, y, c = tm // 4, (tm // 2) % 2, tm % 2

    def at(zz, yy, cc):
        return zz * 4 + yy * 2 + cc

    def slot(zz, yy, cc):
        return zz * 4 + cc * 2 + yy

    def to(index, other=None):
        return (index, x if other is None else other)

    y_peer, c_peer = at(z, 1 - y, c), at(z, y, 1 - c)

    def send(src, dst, ss, rs, dev):
        return pltpu.make_async_remote_copy(
            src_ref=src, dst_ref=dst, send_sem=ss, recv_sem=rs, device_id=dev, device_id_type=MESH
        )

    inner = jnp.logical_or(z == 1, z == 2)
    outer = jnp.logical_or(z == 0, z == 3)

    def w_z(part, d):
        if d == 0:
            src, dst, t = w.at[part], wbuf.at[part, c, y, z], flip(z, 1)
        else:
            near = z // 2
            src = wbuf.at[part, c, y, pl.ds(2 * (near if d == 1 else 1 - near), 2)]
            dst, t = src, (3 - z if d == 1 else flip(z, 1))
        dev = to(at(t, y, c))
        return send(src, dst, wz_s.at[part, d], wz_r.at[part, d], dev)

    def w_y(part):
        ref = wbuf.at[part, c, y]
        return send(ref, ref, wy_s.at[part], wy_r.at[part], to(y_peer))

    def w_c(part):
        ref = wbuf.at[part, c]
        return send(ref, ref, wc_s.at[part], wc_r.at[part], to(c_peer))

    def kv_z(d, j):
        t = flip(z, d)
        dst = kvbuf.at[slot(z, y, c), j]
        return send(kvs.at[t, j], dst, kz_s.at[d, j], kz_r.at[d, j], to(at(t, y, c)))

    def kv_y(d, j):
        ref = kvbuf.at[slot(flip(z, d), y, c), j]
        return send(ref, ref, ky_s.at[d, j], ky_r.at[d, j], to(y_peer))

    def kv_c(d, j):
        ref = kvbuf.at[pl.ds(slot(flip(z, d), 0, c), 2), j]
        return send(ref, ref, kc_s.at[d, j], kc_r.at[d, j], to(c_peer))

    def q_z(d):
        t = flip(z, d)
        return send(qs.at[t], qbuf.at[z], qz_s.at[d], qz_r.at[d], to(at(t, y, c)))

    def o_copy(d, k):
        t = flip(z, d)
        xx = x if k == 0 else 1 - x
        return send(
            ost.at[t, xx], obuf.at[x * ZS + z], o_s.at[d, k], o_r.at[d, k], to(at(t, y, c), xx)
        )

    def p_z(d):
        ref = wobuf.at[c, y, x, z]
        return send(ref, ref, p_s.at[d], p_r.at[d], to(at(flip(z, d), y, c)))

    def p_x():
        ref = wobuf.at[c, y, x]
        return send(ref, ref, p_s.at[4], p_r.at[4], to(tm, 1 - x))

    def p_y():
        ref = wobuf.at[c, y]
        return send(ref, ref, p_s.at[5], p_r.at[5], to(y_peer))

    def p_c():
        ref = wobuf.at[c]
        return send(ref, ref, p_s.at[6], p_r.at[6], to(c_peer))

    partners = [to(at(flip(z, d), y, c)) for d in (1, 2, 3)] + [to(y_peer), to(c_peer)]
    partners += [to(at(flip(z, d), y, c), 1 - x) for d in range(4)]
    barrier = pltpu.get_barrier_semaphore()
    for dev in partners:
        pl.semaphore_signal(barrier, inc=1, device_id=dev, device_id_type=MESH)
    pl.semaphore_wait(barrier, len(partners))

    for part in range(3):
        w_z(part, 0).start()
    for part in range(3):
        wbuf[part, c, y, z] = w[part]
    wobuf[c, y, x, z] = w_out[...]

    log2e = math.log2(math.e)
    slope = slopes[z] * log2e

    def z_near(part):
        w_z(part, 0).wait_recv()

        @pl.when(inner)
        def _():
            w_z(part, 1).start()

    def z_arrived(part):
        @pl.when(inner)
        def _():
            w_z(part, 1).wait_recv()
            w_z(part, 2).start()

        @pl.when(outer)
        def _():
            w_z(part, 2).wait_recv()

        w_y(part).start()

    def y_arrived(part):
        w_y(part).wait_recv()
        w_c(part).start()

    def project(part):
        w_c(part).wait_recv()
        weights = jnp.concatenate(
            [wbuf[part, n % 2, (n // 2) % 2, n // 4] for n in range(blocks)], axis=0
        )
        return jnp.dot(normed[...], weights, preferred_element_type=F32)

    z_near(0)
    z_near(1)
    z_near(2)
    wide = frames[...].astype(F32)
    inverse_root = lax.rsqrt(jnp.mean(wide * wide, axis=-1, keepdims=True) + 1e-06)
    normed[...] = (wide * inverse_root * gain[...]).astype(BF16)

    z_arrived(0)
    ii = lax.broadcasted_iota(jnp.int32, (rows, rows), 0)
    jj = lax.broadcasted_iota(jnp.int32, (rows, rows), 1)
    lin = (ii - jj).astype(F32) * slope
    tiles[0] = -jnp.abs(lin)
    tiles[1] = -lin
    tiles[2] = jnp.abs(lin)
    tiles[3] = lin
    acc[...] = jnp.zeros_like(acc)
    peak[...] = jnp.full_like(peak, -1e30)
    z_arrived(1)
    y_arrived(0)
    z_arrived(2)
    for d in (2, 3, 1):
        p_z(d).start()
    res = (project(0) * (hd ** -0.5 * log2e)).astype(BF16)
    for h in range(ZS):
        qs[h] = res[:, h * hd:(h + 1) * hd]
    for d in (2, 3, 1):
        q_z(d).start()
    qbuf[z] = qs[z]
    mine = slot(z, y, c)
    for part in (1, 2):
        y_arrived(part)
        res = project(part)
        for h in range(ZS):
            piece = res[:, h * hd:(h + 1) * hd]
            if part == 1:
                for a in range(0, rows, hd):
                    kvs[h, 0, a:a + hd, :] = piece[a:a + hd, :].T.astype(BF16)
            else:
                kvs[h, 1] = piece.astype(BF16)
        for d in (2, 1):
            kv_z(d, part - 1).start()
        kvbuf[mine, part - 1] = kvs[z, part - 1]
        kv_y(0, part - 1).start()
    for j in range(2):
        kv_y(0, j).wait_recv()
        kv_c(0, j).start()
    kv_z(2, 0).wait_send()
    kv_z(3, 0).start()

    ones = jnp.ones((rows, hd), BF16)

    wide_rows = 2 * rows

    def step(t, carry):
        d, i = t // 2, t % 2
        zk = flip(z, d)
        g = jnp.where(d == 3, 1 - i, i)
        first = 2 * ((z // 2 + g) % 2)
        place = pl.ds(pl.multiple_of(first * rows, wide_rows), wide_rows)

        @pl.when(t == 0)
        def _():
            q_z(1).wait_recv()
            kv_z(2, 1).wait_send()
            kv_z(3, 1).start()

        @pl.when(t == 1)
        def _():
            q_z(2).wait_recv()
            q_z(3).wait_recv()

        @pl.when(i == 0)
        def _():
            kv_c(d, 0).wait_recv()
            kv_c(d, 1).wait_recv()

        @pl.when(jnp.logical_and(d < 3, i == 0))
        def _():
            for j in range(2):
                kv_z(d + 1, j).wait_recv()
                kv_y(d + 1, j).start()

        @pl.when(jnp.logical_and(d < 3, i == 1))
        def _():
            for j in range(2):
                kv_y(d + 1, j).wait_recv()
                kv_c(d + 1, j).start()

        @pl.when(t == 2)
        def _():
            for n in (1, 2, 3):
                p_z(n).wait_recv()
            p_x().start()

        @pl.when(t == 4)
        def _():
            p_x().wait_recv()
            p_y().start()

        @pl.when(t == 6)
        def _():
            p_y().wait_recv()
            p_c().start()

        def offset(n, k):
            delta = (at(first + n, y, c) - at(zk, k % 2, k // 2) + blocks) % blocks
            middle = blocks // 2
            kind = jnp.where(
                delta == 0, 0, jnp.where(delta < middle, 1, jnp.where(delta == middle, 2, 3))
            )
            far = jnp.where(delta <= middle, delta, blocks - delta) * rows
            return kind, -slope * far.astype(F32)

        offsets = [[offset(n, k) for k in range(4)] for n in range(2)]
        query = qbuf[pl.ds(first, 2)].reshape(wide_rows, hd)
        scores, tops = [], [None, None]
        for k in range(4):
            keys = kvbuf[zk * 4 + k, 0]
            keys = jnp.concatenate([keys[a:a + hd] for a in range(0, rows, hd)], axis=1)
            both = jnp.dot(query, keys, preferred_element_type=F32)
            parts = []
            for n in range(2):
                kind, base = offsets[n][k]
                s = both[n * rows:(n + 1) * rows] + tiles[kind]
                parts.append(s)
                m = s[:, :hd]
                for a in range(hd, rows, hd):
                    m = jnp.maximum(m, s[:, a:a + hd])
                m = m + base
                tops[n] = m if k == 0 else jnp.maximum(tops[n], m)
            scores.append(parts)
        old = peak[place, :]
        top = jnp.concatenate([jnp.max(m, axis=-1, keepdims=True) for m in tops], axis=0)
        new = jnp.maximum(old, top)
        peak[place, :] = new
        shrink = jnp.exp2(old - new)
        total = acc[place, :] * jnp.concatenate([shrink, shrink], axis=1)
        cols = [new[:rows, :1], new[rows:, :1]]
        for k in range(4):
            p = [jnp.exp2(scores[k][n] - (cols[n] - offsets[n][k][1])).astype(BF16) for n in range(2)]
            v = jnp.concatenate([kvbuf[zk * 4 + k, 1], ones], axis=1)
            total = total + jnp.dot(
                jnp.concatenate(p, axis=0), v, preferred_element_type=F32
            )
        acc[place, :] = total

        @pl.when(d == 3)
        def _():
            for n in range(2):
                for s in range(2):
                    start = pl.multiple_of((first + n) * rows + s * half, half)
                    val = acc[pl.ds(start, half), :]
                    ost[first + n, s] = (val[:, :hd] / val[:, hd:]).astype(BF16)

        @pl.when(jnp.logical_and(d == 3, g == 1))
        def _():
            for e in (2, 3):
                o_copy(e, 0).start()
                o_copy(e, 1).start()

        @pl.when(jnp.logical_and(d == 3, g == 0))
        def _():
            o_copy(1, 0).start()
            o_copy(1, 1).start()
            o_copy(0, 1).start()

        return carry

    lax.fori_loop(0, 8, step, 0)

    p_c().wait_recv()
    obuf[x * ZS + z] = ost[z, x]
    for d in (3, 2, 1, 0):
        o_copy(d, 1).wait_recv()
        if d:
            o_copy(d, 0).wait_recv()
    total = None
    for g in range(2):
        mixed = jnp.concatenate([obuf[g * ZS + n] for n in range(ZS)], axis=1)
        weights = jnp.concatenate(
            [wobuf[n % 2, (n // 2) % 2, g, n // 4] for n in range(blocks)], axis=0
        )
        part = lax.dot_general(
            mixed, weights, (((1,), (1,)), ((), ())), preferred_element_type=F32
        )
        total = part if total is None else total + part
    out[...] = total.astype(BF16)

    for part in range(3):
        w_z(part, 0).wait_send()

        @pl.when(inner)
        def _():
            w_z(part, 1).wait_send()
            w_z(part, 2).wait_send()

        w_y(part).wait_send()
        w_c(part).wait_send()
    for d in range(4):
        if d:
            if d != 2:
                kv_z(d, 0).wait_send()
                kv_z(d, 1).wait_send()
            q_z(d).wait_send()
            p_z(d).wait_send()
            o_copy(d, 0).wait_send()
        for j in range(2):
            kv_y(d, j).wait_send()
            kv_c(d, j).wait_send()
        o_copy(d, 1).wait_send()
    p_x().wait_send()
    p_y().wait_send()
    p_c().wait_send()


def local_planes(frames, norm_gain, w_qkv, slopes, w_out):
    rows, width = frames.shape
    blocks = lax.axis_size("tm")
    heads = slopes.shape[0]
    hd = w_qkv.shape[2] // heads
    total = heads * lax.axis_size("head")
    half = rows // 2
    dma = pltpu.SemaphoreType.DMA
    vmem = pl.BlockSpec(memory_space=pltpu.VMEM)
    return pl.pallas_call(
        kernel,
        out_shape=jax.ShapeDtypeStruct((half, width), BF16),
        in_specs=[vmem, vmem, vmem, pl.BlockSpec(memory_space=pltpu.SMEM), vmem],
        out_specs=vmem,
        scratch_shapes=[
            pltpu.VMEM((3, 2, 2, ZS) + w_qkv.shape[1:], BF16),
            pltpu.VMEM((blocks, 2, rows, hd), BF16),
            pltpu.VMEM((ZS, rows, hd), BF16),
            pltpu.VMEM((ZS, 2, rows, hd), BF16),
            pltpu.VMEM((ZS, rows, hd), BF16),
            pltpu.VMEM((total, half, hd), BF16),
            pltpu.VMEM((ZS, 2, half, hd), BF16),
            pltpu.VMEM((rows, width), BF16),
            pltpu.VMEM((4, rows, rows), F32),
            pltpu.VMEM((ZS * rows, 2 * hd), F32),
            pltpu.VMEM((ZS * rows, hd), F32),
            pltpu.VMEM((2, 2, 2, ZS, w_out.shape[1], w_out.shape[0]), BF16),
        ] + [
            dma((3, 4)), dma((3, 4)), dma((3,)), dma((3,)), dma((3,)), dma((3,)),
            dma((4, 2)), dma((4, 2)), dma((4, 2)), dma((4, 2)), dma((4, 2)), dma((4, 2)),
            dma((4,)), dma((4,)), dma((4, 2)), dma((4, 2)), dma((7,)), dma((7,)),
        ],
        compiler_params=pltpu.CompilerParams(
            collective_id=0, has_side_effects=True, vmem_limit_bytes=56 * 1024 * 1024
        ),
        cost_estimate=pl.CostEstimate(
            flops=11 * 10 ** 9, bytes_accessed=6 * 10 ** 6, transcendentals=17 * 10 ** 6
        ),
    )(frames, norm_gain.reshape(1, -1), w_qkv, slopes, w_out.T)


def local(frames, norm_gain, w_qkv, slopes, w_out):
    frame_count = frames.shape[0]
    local_heads = slopes.shape[0]
    head_size = w_qkv.shape[2] // local_heads
    tm_count = lax.axis_size("tm")
    clip_len = frame_count * tm_count
    me_tm = lax.axis_index("tm")
    scale = head_size ** (-0.5)
    wide = frames.astype(F32)
    mean_square = jnp.mean(wide * wide, axis=-1, keepdims=True)
    inverse_root = lax.rsqrt(mean_square + 1e-06)
    normed = (wide * inverse_root * norm_gain).astype(BF16)
    projected = jnp.einsum(
        "rd,cde->cre",
        normed,
        lax.all_gather(w_qkv, "tm", axis=1, tiled=True),
        preferred_element_type=F32,
    ).astype(BF16)
    query, keyed, valued = (
        projected[n].reshape(frame_count, local_heads, head_size) for n in range(3)
    )
    row_pos = me_tm * frame_count + jnp.arange(frame_count, dtype=jnp.int32)
    key_piece = lax.all_gather(keyed, "tm", axis=0, tiled=True)
    scores = jnp.einsum("qhd,khd->hqk", query, key_piece, preferred_element_type=F32) * scale
    key_pos = jnp.arange(key_piece.shape[0], dtype=jnp.int32)
    differ = (key_pos[None, :] - row_pos[:, None]) % clip_len
    distance = jnp.minimum(differ, clip_len - differ).astype(F32)
    scores = scores - slopes[:, None, None] * distance[None, :, :]
    expo = jnp.exp(scores - jnp.max(scores, axis=-1, keepdims=True))
    totals = jnp.sum(expo, axis=-1)
    accum = jnp.einsum(
        "hqk,khd->hqd",
        expo.astype(BF16),
        lax.all_gather(valued, "tm", axis=0, tiled=True),
        preferred_element_type=F32,
    )
    mixed = (accum / totals[:, :, None]).astype(BF16)
    mixed = jnp.transpose(mixed, (1, 0, 2)).reshape(frame_count, local_heads * head_size)
    out_local = lax.all_gather(w_out, "tm", axis=1, tiled=True)
    return lax.psum_scatter(
        jnp.dot(mixed, out_local, preferred_element_type=F32).astype(BF16),
        "head",
        scatter_dimension=0,
        tiled=True,
    )


def solution(mesh):
    in_specs = (P("tm", None), P(), P(None, "tm", "head"), P("head"), P("head", "tm"))
    out_specs = P(("tm", "head"), None)
    planes = mesh.shape["tm"] == 4 * ZS and mesh.shape["head"] == 2
    return jax.shard_map(
        local_planes if planes else local,
        mesh=mesh, in_specs=in_specs, out_specs=out_specs, check_vma=False,
    )
```

```python
import math
import jax
import jax.numpy as jnp
from jax import lax
from jax.experimental import pallas as pl
from jax.experimental.pallas import tpu as pltpu
from jax.sharding import PartitionSpec as P

MESH = pl.DeviceIdType.MESH
ZS = 4
F32 = jnp.float32
BF16 = jnp.bfloat16


def flip(z, d):
    lo, hi = z % 2, z // 2
    dlo, dhi = d % 2, d // 2
    return (lo + dlo) % 2 + 2 * ((hi + dhi) % 2)


def kernel(
    frames, gain, w, slopes, w_out, out,
    wbuf, kvbuf, qbuf, kvs, qs, obuf, ost, normed, tiles, acc, peak, wobuf,
    wz_s, wz_r, wy_s, wy_r, wc_s, wc_r,
    kz_s, kz_r, ky_s, ky_r, kc_s, kc_r,
    qz_s, qz_r, o_s, o_r, p_s, p_r,
):
    rows, width = frames.shape
    hd = kvbuf.shape[-1]
    half = rows // 2
    blocks = kvbuf.shape[0]
    tm = lax.axis_index("tm")
    x = lax.axis_index("head")
    z, y, c = tm // 4, (tm // 2) % 2, tm % 2

    def at(zz, yy, cc):
        return zz * 4 + yy * 2 + cc

    def slot(zz, yy, cc):
        return zz * 4 + cc * 2 + yy

    def to(index, other=None):
        return (index, x if other is None else other)

    y_peer, c_peer = at(z, 1 - y, c), at(z, y, 1 - c)

    def send(src, dst, ss, rs, dev):
        return pltpu.make_async_remote_copy(
            src_ref=src, dst_ref=dst, send_sem=ss, recv_sem=rs, device_id=dev, device_id_type=MESH
        )

    def w_z(part, d):
        dev = to(at(flip(z, d), y, c))
        return send(w.at[part], wbuf.at[part, c, y, z], wz_s.at[part, d], wz_r.at[part, d], dev)

    def w_y(part):
        ref = wbuf.at[part, c, y]
        return send(ref, ref, wy_s.at[part], wy_r.at[part], to(y_peer))

    def w_c(part):
        ref = wbuf.at[part, c]
        return send(ref, ref, wc_s.at[part], wc_r.at[part], to(c_peer))

    def kv_z(d, j):
        t = flip(z, d)
        dst = kvbuf.at[slot(z, y, c), j]
        return send(kvs.at[t, j], dst, kz_s.at[d, j], kz_r.at[d, j], to(at(t, y, c)))

    def kv_y(d, j):
        ref = kvbuf.at[slot(flip(z, d), y, c), j]
        return send(ref, ref, ky_s.at[d, j], ky_r.at[d, j], to(y_peer))

    def kv_c(d, j):
        ref = kvbuf.at[pl.ds(slot(flip(z, d), 0, c), 2), j]
        return send(ref, ref, kc_s.at[d, j], kc_r.at[d, j], to(c_peer))

    def q_z(d):
        t = flip(z, d)
        return send(qs.at[t], qbuf.at[z], qz_s.at[d], qz_r.at[d], to(at(t, y, c)))

    def o_copy(d, k):
        t = flip(z, d)
        xx = x if k == 0 else 1 - x
        return send(
            ost.at[t, xx], obuf.at[x * ZS + z], o_s.at[d, k], o_r.at[d, k], to(at(t, y, c), xx)
        )

    def p_z(d):
        ref = wobuf.at[c, y, x, z]
        return send(ref, ref, p_s.at[d], p_r.at[d], to(at(flip(z, d), y, c)))

    def p_x():
        ref = wobuf.at[c, y, x]
        return send(ref, ref, p_s.at[4], p_r.at[4], to(tm, 1 - x))

    def p_y():
        ref = wobuf.at[c, y]
        return send(ref, ref, p_s.at[5], p_r.at[5], to(y_peer))

    def p_c():
        ref = wobuf.at[c]
        return send(ref, ref, p_s.at[6], p_r.at[6], to(c_peer))

    partners = [to(at(flip(z, d), y, c)) for d in (1, 2, 3)] + [to(y_peer), to(c_peer)]
    partners += [to(at(flip(z, d), y, c), 1 - x) for d in range(4)]
    barrier = pltpu.get_barrier_semaphore()
    for dev in partners:
        pl.semaphore_signal(barrier, inc=1, device_id=dev, device_id_type=MESH)
    pl.semaphore_wait(barrier, len(partners))

    for part in (0, 1):
        for d in (1, 2, 3):
            w_z(part, d).start()
    for part in range(3):
        wbuf[part, c, y, z] = w[part]
    wobuf[c, y, x, z] = w_out[...]

    wide = frames[...].astype(F32)
    inverse_root = lax.rsqrt(jnp.mean(wide * wide, axis=-1, keepdims=True) + 1e-06)
    normed[...] = (wide * inverse_root * gain[...]).astype(BF16)

    log2e = math.log2(math.e)
    slope = slopes[z] * log2e

    def z_arrived(part):
        for d in (1, 2, 3):
            w_z(part, d).wait_recv()
        w_y(part).start()

    def y_arrived(part):
        w_y(part).wait_recv()
        w_c(part).start()

    def project(part):
        w_c(part).wait_recv()
        weights = jnp.concatenate(
            [wbuf[part, n % 2, (n // 2) % 2, n // 4] for n in range(blocks)], axis=0
        )
        return jnp.dot(normed[...], weights, preferred_element_type=F32)

    z_arrived(0)
    for d in (1, 2, 3):
        w_z(2, d).start()
    ii = lax.broadcasted_iota(jnp.int32, (rows, rows), 0)
    jj = lax.broadcasted_iota(jnp.int32, (rows, rows), 1)
    lin = (ii - jj).astype(F32) * slope
    tiles[0] = -jnp.abs(lin)
    tiles[1] = -lin
    tiles[2] = jnp.abs(lin)
    tiles[3] = lin
    acc[...] = jnp.zeros_like(acc)
    peak[...] = jnp.full_like(peak, -1e30)
    z_arrived(1)
    y_arrived(0)
    z_arrived(2)
    res = (project(0) * (hd ** -0.5 * log2e)).astype(BF16)
    for h in range(ZS):
        qs[h] = res[:, h * hd:(h + 1) * hd]
    for d in (1, 2, 3):
        q_z(d).start()
    qbuf[z] = qs[z]
    mine = slot(z, y, c)
    for part in (1, 2):
        y_arrived(part)
        res = project(part)
        for h in range(ZS):
            piece = res[:, h * hd:(h + 1) * hd]
            if part == 1:
                for a in range(0, rows, hd):
                    kvs[h, 0, a:a + hd, :] = piece[a:a + hd, :].T.astype(BF16)
            else:
                kvs[h, 1] = piece.astype(BF16)
        for d in (1, 2):
            kv_z(d, part - 1).start()
        kvbuf[mine, part - 1] = kvs[z, part - 1]
        kv_y(0, part - 1).start()
    for d in (1, 2, 3):
        p_z(d).start()
    for j in range(2):
        kv_y(0, j).wait_recv()
        kv_c(0, j).start()

    ones = jnp.ones((rows, hd), BF16)

    def step(t, carry):
        d, i = t // 4, t % 4
        zk = flip(z, d)
        e = jnp.where(d == 3, 3 - i, i)
        zq = flip(z, e)

        @pl.when(i == 0)
        def _():
            kv_c(d, 0).wait_recv()
            kv_c(d, 1).wait_recv()

        @pl.when(jnp.logical_and(d == 0, i > 0))
        def _():
            q_z(i).wait_recv()

        @pl.when(jnp.logical_and(d < 3, i == 1))
        def _():
            for j in range(2):
                kv_z(d + 1, j).wait_recv()
                kv_y(d + 1, j).start()

        @pl.when(t == 1)
        def _():
            kv_z(3, 0).start()
            kv_z(3, 1).start()

        @pl.when(jnp.logical_and(d < 3, i == 3))
        def _():
            for j in range(2):
                kv_y(d + 1, j).wait_recv()
                kv_c(d + 1, j).start()

        @pl.when(t == 4)
        def _():
            for n in (1, 2, 3):
                p_z(n).wait_recv()
            p_x().start()

        @pl.when(t == 8)
        def _():
            p_x().wait_recv()
            p_y().start()

        @pl.when(t == 12)
        def _():
            p_y().wait_recv()
            p_c().start()

        me = at(zq, y, c)
        kinds, bases = [], []
        for k in range(4):
            delta = (me - at(zk, k % 2, k // 2) + blocks) % blocks
            middle = blocks // 2
            kind = jnp.where(
                delta == 0, 0, jnp.where(delta < middle, 1, jnp.where(delta == middle, 2, 3))
            )
            kinds.append(kind)
            far = jnp.where(delta <= middle, delta, blocks - delta) * rows
            bases.append(-slope * far.astype(F32))
        def score(r, k):
            keys = kvbuf[zk * 4 + k, 0]
            keys = jnp.concatenate([keys[a:a + hd] for a in range(0, rows, hd)], axis=1)
            s = jnp.dot(qbuf[zq, r:r + half, :], keys, preferred_element_type=F32)
            s = s + tiles[kinds[k], r:r + half, :]
            m = s[:, :hd]
            for a in range(hd, rows, hd):
                m = jnp.maximum(m, s[:, a:a + hd])
            return s, m + bases[k]

        def begin(r, tops):
            place = pl.ds(pl.multiple_of(zq * rows + r, half), half)
            top = jnp.maximum(jnp.maximum(tops[0], tops[1]), jnp.maximum(tops[2], tops[3]))
            old = peak[place, :]
            new = jnp.maximum(old, jnp.max(top, axis=-1, keepdims=True))
            peak[place, :] = new
            shrink = jnp.exp2(old - new)
            return new[:, :1], acc[place, :] * jnp.concatenate([shrink, shrink], axis=1)

        def add(total, s, col, k):
            p = jnp.exp2((s - (col - bases[k])).astype(BF16))
            v = jnp.concatenate([kvbuf[zk * 4 + k, 1], ones], axis=1)
            return total + jnp.dot(p, v, preferred_element_type=F32)

        def finish(r, total):
            acc[pl.ds(pl.multiple_of(zq * rows + r, half), half), :] = total

        first = [score(0, k) for k in range(4)]
        col, total = begin(0, [m for _, m in first])
        second = []
        for k in range(4):
            second.append(score(half, k))
            total = add(total, first[k][0], col, k)
        finish(0, total)
        col, total = begin(half, [m for _, m in second])
        for k in range(4):
            total = add(total, second[k][0], col, k)
        finish(half, total)

        @pl.when(d == 3)
        def _():
            for s in range(2):
                place = pl.ds(pl.multiple_of(zq * rows + s * half, half), half)
                val = acc[place, :]
                ost[zq, s] = (val[:, :hd] / val[:, hd:]).astype(BF16)
            o_copy(e, 1).start()

        @pl.when(jnp.logical_and(d == 3, e > 0))
        def _():
            o_copy(e, 0).start()

        return carry

    lax.fori_loop(0, 16, step, 0)

    p_c().wait_recv()
    obuf[x * ZS + z] = ost[z, x]
    for d in (3, 2, 1, 0):
        o_copy(d, 1).wait_recv()
        if d:
            o_copy(d, 0).wait_recv()
    total = None
    for g in range(2):
        mixed = jnp.concatenate([obuf[g * ZS + n] for n in range(ZS)], axis=1)
        weights = jnp.concatenate(
            [wobuf[n % 2, (n // 2) % 2, g, n // 4] for n in range(blocks)], axis=0
        )
        part = lax.dot_general(
            mixed, weights, (((1,), (1,)), ((), ())), preferred_element_type=F32
        )
        total = part if total is None else total + part
    out[...] = total.astype(BF16)

    for part in range(3):
        for d in (1, 2, 3):
            w_z(part, d).wait_send()
        w_y(part).wait_send()
        w_c(part).wait_send()
    for d in range(4):
        if d:
            kv_z(d, 0).wait_send()
            kv_z(d, 1).wait_send()
            q_z(d).wait_send()
            p_z(d).wait_send()
            o_copy(d, 0).wait_send()
        for j in range(2):
            kv_y(d, j).wait_send()
            kv_c(d, j).wait_send()
        o_copy(d, 1).wait_send()
    p_x().wait_send()
    p_y().wait_send()
    p_c().wait_send()


def local_planes(frames, norm_gain, w_qkv, slopes, w_out):
    rows, width = frames.shape
    blocks = lax.axis_size("tm")
    heads = slopes.shape[0]
    hd = w_qkv.shape[2] // heads
    total = heads * lax.axis_size("head")
    half = rows // 2
    dma = pltpu.SemaphoreType.DMA
    vmem = pl.BlockSpec(memory_space=pltpu.VMEM)
    return pl.pallas_call(
        kernel,
        out_shape=jax.ShapeDtypeStruct((half, width), BF16),
        in_specs=[vmem, vmem, vmem, pl.BlockSpec(memory_space=pltpu.SMEM), vmem],
        out_specs=vmem,
        scratch_shapes=[
            pltpu.VMEM((3, 2, 2, ZS) + w_qkv.shape[1:], BF16),
            pltpu.VMEM((blocks, 2, rows, hd), BF16),
            pltpu.VMEM((ZS, rows, hd), BF16),
            pltpu.VMEM((ZS, 2, rows, hd), BF16),
            pltpu.VMEM((ZS, rows, hd), BF16),
            pltpu.VMEM((total, half, hd), BF16),
            pltpu.VMEM((ZS, 2, half, hd), BF16),
            pltpu.VMEM((rows, width), BF16),
            pltpu.VMEM((4, rows, rows), F32),
            pltpu.VMEM((ZS * rows, 2 * hd), F32),
            pltpu.VMEM((ZS * rows, hd), F32),
            pltpu.VMEM((2, 2, 2, ZS, w_out.shape[1], w_out.shape[0]), BF16),
        ] + [
            dma((3, 4)), dma((3, 4)), dma((3,)), dma((3,)), dma((3,)), dma((3,)),
            dma((4, 2)), dma((4, 2)), dma((4, 2)), dma((4, 2)), dma((4, 2)), dma((4, 2)),
            dma((4,)), dma((4,)), dma((4, 2)), dma((4, 2)), dma((7,)), dma((7,)),
        ],
        compiler_params=pltpu.CompilerParams(
            collective_id=0, has_side_effects=True, vmem_limit_bytes=56 * 1024 * 1024
        ),
        cost_estimate=pl.CostEstimate(
            flops=11 * 10 ** 9, bytes_accessed=6 * 10 ** 6, transcendentals=17 * 10 ** 6
        ),
    )(frames, norm_gain.reshape(1, -1), w_qkv, slopes, w_out.T)


def local(frames, norm_gain, w_qkv, slopes, w_out):
    frame_count = frames.shape[0]
    local_heads = slopes.shape[0]
    head_size = w_qkv.shape[2] // local_heads
    tm_count = lax.axis_size("tm")
    clip_len = frame_count * tm_count
    me_tm = lax.axis_index("tm")
    scale = head_size ** (-0.5)
    wide = frames.astype(F32)
    mean_square = jnp.mean(wide * wide, axis=-1, keepdims=True)
    inverse_root = lax.rsqrt(mean_square + 1e-06)
    normed = (wide * inverse_root * norm_gain).astype(BF16)
    projected = jnp.einsum(
        "rd,cde->cre",
        normed,
        lax.all_gather(w_qkv, "tm", axis=1, tiled=True),
        preferred_element_type=F32,
    ).astype(BF16)
    query, keyed, valued = (
        projected[n].reshape(frame_count, local_heads, head_size) for n in range(3)
    )
    row_pos = me_tm * frame_count + jnp.arange(frame_count, dtype=jnp.int32)
    key_piece = lax.all_gather(keyed, "tm", axis=0, tiled=True)
    scores = jnp.einsum("qhd,khd->hqk", query, key_piece, preferred_element_type=F32) * scale
    key_pos = jnp.arange(key_piece.shape[0], dtype=jnp.int32)
    differ = (key_pos[None, :] - row_pos[:, None]) % clip_len
    distance = jnp.minimum(differ, clip_len - differ).astype(F32)
    scores = scores - slopes[:, None, None] * distance[None, :, :]
    expo = jnp.exp(scores - jnp.max(scores, axis=-1, keepdims=True))
    totals = jnp.sum(expo, axis=-1)
    accum = jnp.einsum(
        "hqk,khd->hqd",
        expo.astype(BF16),
        lax.all_gather(valued, "tm", axis=0, tiled=True),
        preferred_element_type=F32,
    )
    mixed = (accum / totals[:, :, None]).astype(BF16)
    mixed = jnp.transpose(mixed, (1, 0, 2)).reshape(frame_count, local_heads * head_size)
    out_local = lax.all_gather(w_out, "tm", axis=1, tiled=True)
    return lax.psum_scatter(
        jnp.dot(mixed, out_local, preferred_element_type=F32).astype(BF16),
        "head",
        scatter_dimension=0,
        tiled=True,
    )


def solution(mesh):
    in_specs = (P("tm", None), P(), P(None, "tm", "head"), P("head"), P("head", "tm"))
    out_specs = P(("tm", "head"), None)
    planes = mesh.shape["tm"] == 4 * ZS and mesh.shape["head"] == 2
    return jax.shard_map(
        local_planes if planes else local,
        mesh=mesh, in_specs=in_specs, out_specs=out_specs, check_vma=False,
    )
```
